32 devices in a mesh: geom: 2 (over x), op: 8 (over z, y), col: 2 (over core).
Axes of the slice: x: 2, y: 2, z: 4, core: 2. Of those that a mesh axis runs over, the one named last changes fastest.
Arguments:
- wave_coef: float32 [2048, 1024], P('geom', 'col'), parts along dimension 0, may hold values from -6 to 6
- diag_energy: float32 [2048, 1024], P('geom', 'col'), parts along dimension 0, may hold values from -4 to 4
- left_block: bfloat16 [32, 1024, 1024], P(('geom', 'op')), parts along dimension 0, may hold values from -0.1875 to 0.1875
- right_block: bfloat16 [32, 1024, 1024], P(('geom', 'op'), None, 'col'), parts along dimension 0, may hold values from -0.1875 to 0.1875
- block_mask: int32 [32, 8, 8], P(('geom', 'op')), parts along dimension 0, may hold values 0 or 1
Outputs:
- new_wave: float32 [2048, 1024], P('geom', 'col'), parts along dimension 0
The draws below stay inside these ranges and needn't reach their ends.
There are 2 independent parts, one for each index of `geom`. The reference program is written for one: setup_inputs(seed, part) draws one part's arguments, and reference() takes and returns one part's arrays. A program takes and returns all parts, laid end to end along the dimension named above; each array names one. Nothing has to cross between parts.
All inputs are finite; a program needn't handle non-finite values. No bound on the sum of `block_mask` on one device may be relied on, other than what follows from the above.
Results may differ from the reference program's by a relative error of at most 0.0042.
The reference program's roundings to bfloat16 on the way (of `masked`, `wave` and `inner`) count: a program that leaves them out, or rounds other values in their place, can miss the bound.
Values may be sent and summed in bfloat16 or wider, within the bound.
No kernel may reach another device: no remote copies, remote signals or barrier semaphores. Data moves between devices by JAX's collectives and lax.ppermute only.
A program may use at most 64 MiB of HBM per device.

```python
import jax
import jax.numpy as jnp
from jax import lax

M = 1024
NB = 8
STEPS = 2
PAIRS = 16


def plant(entries, key, low, top_value):
    spot = [jax.random.randint(jax.random.fold_in(key, axis), (), 0, length) for axis, length in enumerate(entries.shape)]
    main_axis = entries.shape.index(max(entries.shape))
    neighbour = spot[:main_axis] + [(spot[main_axis] + 1) % entries.shape[main_axis]] + spot[main_axis + 1:]
    return entries.at[tuple(spot)].set(low).at[tuple(neighbour)].set(top_value)


def block_levels(stream_key, shape, shards, smallest, largest):
    gain, own = 1.0, jax.random.fold_in(stream_key, 6)
    for position, parts in shards:
        steps = jnp.exp(jax.random.uniform(jax.random.fold_in(own, position), (parts,), jnp.float32, smallest / len(shards), largest / len(shards)))
        gain = gain * jnp.repeat(steps, shape[position] // parts).reshape([-1 if axis == position else 1 for axis in range(len(shape))])
    return gain


def normal_values(own_key, dims, scale, bound, shards=(), held_as=jnp.bfloat16):
    drawn = scale * jax.random.normal(own_key, dims, jnp.float32)
    if shards:
        drawn = drawn * block_levels(own_key, dims, shards, -0.22, 0.18)
    return jnp.clip(drawn, -bound, bound).astype(held_as)


def setup_inputs(seed: int = 0, part: int = 0) -> dict:
    splits = jax.random.split(jax.random.key(seed), 6)
    own_keys = jax.random.split(jax.random.fold_in(splits[5], part), 6)
    return {
        "wave_coef": normal_values(own_keys[0], (M, M), 1.0, 6.0, ((1, 2),), jnp.float32),
        "diag_energy": jnp.clip(jax.random.uniform(own_keys[1], (M, M), jnp.float32, -4.0, 4.0) * block_levels(own_keys[1], (M, M), ((1, 2),), -0.4, 0.0), -4.0, 4.0),
        "left_block": normal_values(own_keys[2], (PAIRS, M, M), M ** -0.5, 0.1875, ((0, 8),)),
        "right_block": normal_values(own_keys[3], (PAIRS, M, M), M ** -0.5, 0.1875, ((0, 8), (2, 2))),
        "block_mask": plant((jax.random.randint(own_keys[4], (PAIRS, NB, NB), 0, 2) < 1).astype(jnp.int32), jax.random.fold_in(own_keys[4], 1), 0, 1),
    }


def apply_mask(left_block, block_mask):
    total, width, _ = left_block.shape
    blocks = block_mask.shape[1]
    inside = width // blocks
    grid = left_block.reshape(total, blocks, inside, blocks, inside)
    keep = block_mask.astype(jnp.bfloat16)[:, :, None, :, None]
    return (grid * keep).reshape(total, width, width)

def update(coef, sigma, diag_energy):
    theta = jnp.mean(coef * sigma) / (jnp.mean(coef * coef) + 1e-06)
    spacing = diag_energy - theta
    correction = (sigma - theta * coef) * spacing / jnp.maximum(spacing * spacing, 1.0)
    moved = coef - correction
    return moved * lax.rsqrt(jnp.mean(moved * moved) + 1e-06)

def reference(wave_coef, diag_energy, left_block, right_block, block_mask):
    masked = apply_mask(left_block, block_mask)
    coef = wave_coef
    for step in range(STEPS):
        wave = coef.astype(jnp.bfloat16)

        def add_pair(total, operands):
            left_op, right_op = operands
            inner = jnp.dot(wave, right_op, preferred_element_type=jnp.float32).astype(jnp.bfloat16)
            return (total + jnp.dot(left_op, inner, preferred_element_type=jnp.float32), None)
        sigma, _ = lax.scan(add_pair, jnp.zeros(coef.shape, jnp.float32), (masked, right_block))
        coef = update(coef, sigma, diag_energy)
    return coef
```

```python
import functools

import jax
import jax.numpy as jnp
from jax import lax
from jax.experimental import pallas as pl
from jax.experimental.pallas import tpu as pltpu
from jax.sharding import PartitionSpec as P

STEPS = 2
EPS = 1e-06
TOP = 0.1875
BOTH = ("op", "col")


def any_spec():
    return pl.BlockSpec(memory_space=pl.ANY)


def smem_spec():
    return pl.BlockSpec(memory_space=pltpu.SMEM)


def load(src, dst, sem):
    copy = pltpu.make_async_copy(src, dst, sem)
    copy.start()
    return copy


def mask_rows(mask_ref, left_ref, masked_ref, blocks, first):
    pairs, rows, width = left_ref.shape
    inside = width // blocks
    for k in range(pairs):
        for i in range(rows // inside):
            for j in range(blocks):
                keep = mask_ref[k * blocks * blocks + (first + i) * blocks + j]
                block = left_ref[k, i * inside:(i + 1) * inside, j * inside:(j + 1) * inside]
                masked_ref[i * inside:(i + 1) * inside, k * width + j * inside:k * width + (j + 1) * inside] = (
                    jnp.where(keep != 0, block, jnp.zeros_like(block)))


def first_kernel(count, blocks, place_ref, mask_ref, *refs):
    pieces, (right_ref, left_ref, inner_out, send_out, wave, right, left, inner, masked, sems, out_sem) = (
        refs[:count], refs[count:])
    pairs, width, cols = right.shape
    rows = left.shape[1]
    first = pl.multiple_of(place_ref[0], rows)
    got = []
    for p, piece in enumerate(pieces):
        at = (pl.ds(pl.multiple_of(place_ref[1 + 2 * p], piece.shape[0]), piece.shape[0]),
              pl.ds(pl.multiple_of(place_ref[2 + 2 * p], cols), cols))
        got.append(load(piece, wave.at[at], sems.at[p]))
    rights = [load(right_ref.at[k], right.at[k], sems.at[count + k]) for k in range(pairs)]
    lefts = [load(left_ref.at[k, pl.ds(first, rows)], left.at[k], sems.at[count + pairs + k]) for k in range(pairs)]
    for copy in got:
        copy.wait()
    for k in range(pairs):
        rights[k].wait()
        for r in range(width // rows):
            inner[k * width + r * rows:k * width + (r + 1) * rows, :] = jnp.dot(
                wave[r * rows:(r + 1) * rows, :], right[k], preferred_element_type=jnp.float32).astype(jnp.bfloat16)
    out = load(inner, inner_out, out_sem)
    for copy in lefts:
        copy.wait()
    mask_rows(mask_ref, left, masked, blocks, place_ref[0] // (width // blocks))
    send_out[...] = jnp.dot(masked[...], inner[...], preferred_element_type=jnp.float32)
    out.wait()


def second_kernel(count, blocks, place_ref, mask_ref, *refs):
    pieces, (send_ref, inner_ref, left_ref, keep_out, corr_out, own, send, left, inner, masked, sems) = (
        refs[:count], refs[count:])
    pairs, rows, width = left.shape
    kept = pl.multiple_of(rows - place_ref[0], rows)
    got = [load(inner_ref, inner, sems.at[0])]
    lefts = [load(left_ref.at[k, pl.ds(kept, rows)], left.at[k], sems.at[1 + k]) for k in range(pairs)]
    got.append(load(send_ref, send, sems.at[1 + pairs]))
    for p, piece in enumerate(pieces):
        at = pl.ds(pl.multiple_of(place_ref[1 + 2 * p], piece.shape[0]), piece.shape[0])
        got.append(load(piece, own.at[at], sems.at[2 + pairs + p]))
    for copy in lefts:
        copy.wait()
    mask_rows(mask_ref, left, masked, blocks, (rows - place_ref[0]) // (width // blocks))
    for copy in got:
        copy.wait()
    keep_out[...] = jnp.dot(masked[...], inner[...], preferred_element_type=jnp.float32)
    first = pl.multiple_of(place_ref[0], rows)
    product = (own[pl.ds(first, rows), :].astype(jnp.float32) * send[...]
               + own[pl.ds(kept, rows), :].astype(jnp.float32) * keep_out[...])
    corr_out[...] = jnp.full(corr_out.shape, jnp.sum(product), jnp.float32)


def sigma_halves(place, mask, own, other, right, left, blocks):
    pairs, width, cols = right.shape
    half = width // 2
    sds = jax.ShapeDtypeStruct
    bf16, f32 = jnp.bfloat16, jnp.float32
    pieces = [p.astype(bf16) for p in own] + other
    flops = 2 * pairs * width * cols
    vmem = pltpu.CompilerParams(vmem_limit_bytes=32 * 2 ** 20)
    inner, send = pl.pallas_call(
        functools.partial(first_kernel, len(pieces), blocks),
        out_shape=(sds((pairs * width, cols), bf16), sds((half, cols), f32)),
        in_specs=[smem_spec(), smem_spec()] + [any_spec()] * (len(pieces) + 2),
        out_specs=(any_spec(), pl.BlockSpec(memory_space=pltpu.VMEM)),
        scratch_shapes=[
            pltpu.VMEM((width, width), bf16),
            pltpu.VMEM((pairs, width, cols), bf16),
            pltpu.VMEM((pairs, half, width), bf16),
            pltpu.VMEM((pairs * width, cols), bf16),
            pltpu.VMEM((half, pairs * width), bf16),
            pltpu.SemaphoreType.DMA((len(pieces) + 2 * pairs,)),
            pltpu.SemaphoreType.DMA(()),
        ],
        compiler_params=vmem,
        cost_estimate=pl.CostEstimate(flops=flops * (width + half), bytes_accessed=8 * 2 ** 20, transcendentals=0),
        name="inner_and_sent_half",
    )(place, mask, *pieces, right, left)
    return inner, send


def sigma_kept(place, mask, own, send, inner, left, blocks):
    pairs, width, _ = left.shape
    half, cols = send.shape
    sds = jax.ShapeDtypeStruct
    bf16, f32 = jnp.bfloat16, jnp.float32
    return pl.pallas_call(
        functools.partial(second_kernel, len(own), blocks),
        out_shape=(sds((half, cols), f32), sds((8, 128), f32)),
        in_specs=[smem_spec(), smem_spec()] + [any_spec()] * (len(own) + 3),
        out_specs=(pl.BlockSpec(memory_space=pltpu.VMEM), pl.BlockSpec(memory_space=pltpu.VMEM)),
        scratch_shapes=[
            pltpu.VMEM((width, cols), own[0].dtype),
            pltpu.VMEM((half, cols), f32),
            pltpu.VMEM((pairs, half, width), bf16),
            pltpu.VMEM((pairs * width, cols), bf16),
            pltpu.VMEM((half, pairs * width), bf16),
            pltpu.SemaphoreType.DMA((len(own) + 2 + pairs,)),
        ],
        compiler_params=pltpu.CompilerParams(vmem_limit_bytes=32 * 2 ** 20),
        cost_estimate=pl.CostEstimate(
            flops=2 * pairs * width * cols * half, bytes_accessed=8 * 2 ** 20, transcendentals=0),
        name="kept_half",
    )(place, mask, *own, send, inner, left)


def local(ops, cols, wave_coef, diag_energy, left, right, block_mask):
    f32, f16, bf16 = jnp.float32, jnp.float16, jnp.bfloat16
    pairs, width, _ = left.shape
    own_cols = right.shape[2]
    blocks = block_mask.shape[1]
    cells = float(width * width)
    half, quarter = width // 2, width // 4
    me, core = lax.axis_index("op"), lax.axis_index("col")
    order = ((1, 2), (2, 1))

    def swap(x, stage):
        pairing = []
        for o in range(ops):
            for c in range(cols):
                bit = order[c % 2][stage] if stage < 2 else 1 << stage
                pairing.append((o * cols + c, (o ^ bit) * cols + c))
        return lax.ppermute(x, BOTH, pairing)

    def across(x):
        return lax.ppermute(x, "col", [(c, c ^ 1) for c in range(cols)])

    stages = ops.bit_length() - 1
    low, high = me % 2, (me // 2) % 2

    def bits(c):
        return jnp.where(c == 0, low, high), jnp.where(c == 0, high, low)

    bit0, bit1 = bits(core)
    there0, there1 = bits(1 - core)
    row = bit0 * half + bit1 * quarter
    zero = jnp.zeros((), jnp.int32)

    def quarters(b0, b1):
        return [b0 * half + b1 * quarter, b0 * half + (1 - b1) * quarter,
                (1 - b0) * half + b1 * quarter, (1 - b0) * half + (1 - b1) * quarter]

    sent = (1 - bit0) * half
    mask = block_mask.reshape(-1)
    diag = lax.dynamic_slice(diag_energy, (row, zero), (quarter, own_cols))
    coef = lax.dynamic_slice(wave_coef, (row, zero), (quarter, own_cols))

    reach = float(pairs * ops * width) * TOP * TOP

    own = [wave_coef]
    wave = wave_coef.astype(bf16)
    other = [across(wave)]
    weight = jnp.sum(wave_coef * wave_coef)
    weight = weight + across(weight)
    norm = jnp.ones((), f32)
    for step in range(STEPS):
        if step == 0:
            place = [sent, zero, core * own_cols, zero, (1 - core) * own_cols]
        else:
            place = [sent]
            for c, (b0, b1) in ((core, (bit0, bit1)), (1 - core, (there0, there1))):
                for first in quarters(b0, b1):
                    place += [first, c * own_cols]
        place = jnp.stack(place).astype(jnp.int32)
        inner, send = sigma_halves(place, mask, own, other, right, left, blocks)
        length = jnp.sqrt(weight) + 1e-30
        scale = 32768.0 / (reach * length)
        got = swap((send * scale).astype(f16), 0)
        keep, corr = sigma_kept(place, mask, own, send, inner, left, blocks)
        corr = corr + across(corr)
        corr = corr + swap(corr, 0)
        keep = keep * scale + got.astype(f32)
        send = lax.dynamic_slice(keep, ((1 - bit1) * quarter, zero), (quarter, own_cols)).astype(f16)
        keep = lax.dynamic_slice(keep, (bit1 * quarter, zero), (quarter, own_cols))
        got = swap(send, 1)
        corr = corr + swap(corr, 1)
        keep = keep + got.astype(f32)
        for stage in range(2, stages):
            send = keep.astype(f16)
            got = swap(send, stage)
            corr = corr + swap(corr, stage)
            keep = send.astype(f32) + got.astype(f32)
        sigma = keep * (norm / scale)
        square = norm * norm
        theta = (corr[0, 0] * square / cells) / (weight * square / cells + EPS)
        spacing = diag - theta
        correction = (sigma - theta * coef) * spacing / jnp.maximum(spacing * spacing, 1.0)
        moved = coef - correction
        last = step == STEPS - 1
        if last:
            shrink = 32768.0 / ((1.0 + jnp.abs(theta) + reach) * (length * norm))
            moved = moved * shrink
            piece = moved.astype(f16)
        else:
            piece = moved.astype(bf16)
        weight = jnp.full((8, 128), jnp.sum(moved * moved), f32)
        p1 = swap(piece, 1)
        p2 = swap(piece, 0)
        p3 = swap(p1, 0)
        weight = weight + across(weight)
        weight = weight + swap(weight, 1)
        weight = (weight + swap(weight, 0))[0, 0]
        if not last:
            norm = lax.rsqrt(weight / cells + EPS)
            coef = moved * norm
            own = [piece, p1, p2, p3]
            other = [across(p) for p in own]
        else:
            norm = lax.rsqrt(weight / cells + EPS * shrink * shrink)
            near0, near1 = jnp.where(bit1 == 0, piece, p1), jnp.where(bit1 == 0, p1, piece)
            far0, far1 = jnp.where(bit1 == 0, p2, p3), jnp.where(bit1 == 0, p3, p2)
            full = jnp.concatenate([
                jnp.where(bit0 == 0, near0, far0), jnp.where(bit0 == 0, near1, far1),
                jnp.where(bit0 == 0, far0, near0), jnp.where(bit0 == 0, far1, near1)], axis=0)
            return full.astype(f32) * norm


def solution(mesh):
    in_specs = (
        P("geom", "col"),
        P("geom", "col"),
        P(("geom", "op"), None, None),
        P(("geom", "op"), None, "col"),
        P(("geom", "op"), None, None),
    )
    body = functools.partial(local, mesh.shape["op"], mesh.shape["col"])
    return jax.shard_map(body, mesh=mesh, in_specs=in_specs, out_specs=P("geom", "col"), check_vma=False)
```

```python
import functools

import jax
import jax.numpy as jnp
from jax import lax
from jax.experimental import pallas as pl
from jax.experimental.pallas import tpu as pltpu
from jax.sharding import PartitionSpec as P

STEPS = 2
EPS = 1e-06
TOP = 0.1875
BOTH = ("op", "col")


def any_spec():
    return pl.BlockSpec(memory_space=pl.ANY)


def hbm_spec():
    return pl.BlockSpec(memory_space=pltpu.HBM)


def smem_spec():
    return pl.BlockSpec(memory_space=pltpu.SMEM)


def load(src, dst, sem):
    copy = pltpu.make_async_copy(src, dst, sem)
    copy.start()
    return copy


def mask_rows(mask_ref, left_ref, masked_ref, blocks, first):
    pairs, rows, width = left_ref.shape
    inside = width // blocks
    for k in range(pairs):
        for i in range(rows // inside):
            for j in range(blocks):
                keep = mask_ref[k * blocks * blocks + (first + i) * blocks + j]
                block = left_ref[k, i * inside:(i + 1) * inside, j * inside:(j + 1) * inside]
                masked_ref[i * inside:(i + 1) * inside, k * width + j * inside:k * width + (j + 1) * inside] = (
                    jnp.where(keep != 0, block, jnp.zeros_like(block)))


def first_kernel(count, blocks, place_ref, mask_ref, *refs):
    pieces, (right_ref, left_ref, inner_out, send_out, wave, right, left, inner, masked, sems, out_sem) = (
        refs[:count], refs[count:])
    pairs, width, cols = right.shape
    rows = left.shape[1]
    first = pl.multiple_of(place_ref[0], rows)
    got = []
    for p, piece in enumerate(pieces):
        at = (pl.ds(pl.multiple_of(place_ref[1 + 2 * p], piece.shape[0]), piece.shape[0]),
              pl.ds(pl.multiple_of(place_ref[2 + 2 * p], cols), cols))
        got.append(load(piece, wave.at[at], sems.at[p]))
    rights = [load(right_ref.at[k], right.at[k], sems.at[count + k]) for k in range(pairs)]
    lefts = [load(left_ref.at[k, pl.ds(first, rows)], left.at[k], sems.at[count + pairs + k]) for k in range(pairs)]
    for copy in got:
        copy.wait()
    for k in range(pairs):
        rights[k].wait()
        for r in range(width // rows):
            inner[k * width + r * rows:k * width + (r + 1) * rows, :] = jnp.dot(
                wave[r * rows:(r + 1) * rows, :], right[k], preferred_element_type=jnp.float32).astype(jnp.bfloat16)
    out = load(inner, inner_out, out_sem)
    for copy in lefts:
        copy.wait()
    mask_rows(mask_ref, left, masked, blocks, place_ref[0] // (width // blocks))
    send_out[...] = jnp.dot(masked[...], inner[...], preferred_element_type=jnp.float32)
    out.wait()


def second_kernel(count, blocks, place_ref, mask_ref, *refs):
    pieces, (send_ref, inner_ref, left_ref, keep_out, corr_out, own, send, left, inner, masked, sems) = (
        refs[:count], refs[count:])
    pairs, rows, width = left.shape
    kept = pl.multiple_of(rows - place_ref[0], rows)
    got = [load(inner_ref, inner, sems.at[0])]
    lefts = [load(left_ref.at[k, pl.ds(kept, rows)], left.at[k], sems.at[1 + k]) for k in range(pairs)]
    got.append(load(send_ref, send, sems.at[1 + pairs]))
    for p, piece in enumerate(pieces):
        at = pl.ds(pl.multiple_of(place_ref[1 + 2 * p], piece.shape[0]), piece.shape[0])
        got.append(load(piece, own.at[at], sems.at[2 + pairs + p]))
    for copy in lefts:
        copy.wait()
    mask_rows(mask_ref, left, masked, blocks, (rows - place_ref[0]) // (width // blocks))
    for copy in got:
        copy.wait()
    keep_out[...] = jnp.dot(masked[...], inner[...], preferred_element_type=jnp.float32)
    first = pl.multiple_of(place_ref[0], rows)
    product = (own[pl.ds(first, rows), :].astype(jnp.float32) * send[...]
               + own[pl.ds(kept, rows), :].astype(jnp.float32) * keep_out[...])
    corr_out[0, 0] = jnp.sum(product)


def sigma_halves(place, mask, own, other, right, left, blocks):
    pairs, width, cols = right.shape
    half = width // 2
    sds = jax.ShapeDtypeStruct
    bf16, f32 = jnp.bfloat16, jnp.float32
    pieces = [p.astype(bf16) for p in own] + other
    flops = 2 * pairs * width * cols
    vmem = pltpu.CompilerParams(vmem_limit_bytes=20 * 2 ** 20)
    inner, send = pl.pallas_call(
        functools.partial(first_kernel, len(pieces), blocks),
        out_shape=(sds((pairs * width, cols), bf16), sds((half, cols), f32)),
        in_specs=[smem_spec(), smem_spec()] + [any_spec()] * len(pieces) + [hbm_spec()] * 2,
        out_specs=(any_spec(), pl.BlockSpec(memory_space=pltpu.VMEM)),
        scratch_shapes=[
            pltpu.VMEM((width, width), bf16),
            pltpu.VMEM((pairs, width, cols), bf16),
            pltpu.VMEM((pairs, half, width), bf16),
            pltpu.VMEM((pairs * width, cols), bf16),
            pltpu.VMEM((half, pairs * width), bf16),
            pltpu.SemaphoreType.DMA((len(pieces) + 2 * pairs,)),
            pltpu.SemaphoreType.DMA(()),
        ],
        compiler_params=vmem,
        cost_estimate=pl.CostEstimate(flops=flops * (width + half), bytes_accessed=8 * 2 ** 20, transcendentals=0),
        name="inner_and_sent_half",
    )(place, mask, *pieces, right, left)
    return inner, send


def sigma_kept(place, mask, own, send, inner, left, blocks):
    pairs, width, _ = left.shape
    half, cols = send.shape
    sds = jax.ShapeDtypeStruct
    bf16, f32 = jnp.bfloat16, jnp.float32
    return pl.pallas_call(
        functools.partial(second_kernel, len(own), blocks),
        out_shape=(sds((half, cols), f32), sds((1, 1), f32)),
        in_specs=[smem_spec(), smem_spec()] + [any_spec()] * (len(own) + 2) + [hbm_spec()],
        out_specs=(pl.BlockSpec(memory_space=pltpu.VMEM), smem_spec()),
        scratch_shapes=[
            pltpu.VMEM((width, cols), own[0].dtype),
            pltpu.VMEM((half, cols), f32),
            pltpu.VMEM((pairs, half, width), bf16),
            pltpu.VMEM((pairs * width, cols), bf16),
            pltpu.VMEM((half, pairs * width), bf16),
            pltpu.SemaphoreType.DMA((len(own) + 2 + pairs,)),
        ],
        compiler_params=pltpu.CompilerParams(vmem_limit_bytes=20 * 2 ** 20),
        cost_estimate=pl.CostEstimate(
            flops=2 * pairs * width * cols * half, bytes_accessed=8 * 2 ** 20, transcendentals=0),
        name="kept_half",
    )(place, mask, *own, send, inner, left)


def local(ops, cols, wave_coef, diag_energy, left, right, block_mask):
    f32, f16, bf16 = jnp.float32, jnp.float16, jnp.bfloat16
    pairs, width, _ = left.shape
    own_cols = right.shape[2]
    blocks = block_mask.shape[1]
    cells = float(width * width)
    half, quarter = width // 2, width // 4
    me, core = lax.axis_index("op"), lax.axis_index("col")
    order = ((1, 2), (2, 1))

    def swap(x, stage):
        pairing = []
        for o in range(ops):
            for c in range(cols):
                bit = order[c % 2][stage] if stage < 2 else 1 << stage
                pairing.append((o * cols + c, (o ^ bit) * cols + c))
        return lax.ppermute(x, BOTH, pairing)

    def across(x):
        return lax.ppermute(x, "col", [(c, c ^ 1) for c in range(cols)])

    stages = ops.bit_length() - 1
    low, high = me % 2, (me // 2) % 2

    def bits(c):
        return jnp.where(c == 0, low, high), jnp.where(c == 0, high, low)

    bit0, bit1 = bits(core)
    there0, there1 = bits(1 - core)
    row = bit0 * half + bit1 * quarter
    zero = jnp.zeros((), jnp.int32)

    def quarters(b0, b1):
        return [b0 * half + b1 * quarter, b0 * half + (1 - b1) * quarter,
                (1 - b0) * half + b1 * quarter, (1 - b0) * half + (1 - b1) * quarter]

    sent = (1 - bit0) * half
    mask = block_mask.reshape(-1)
    diag = lax.dynamic_slice(diag_energy, (row, zero), (quarter, own_cols))
    coef = lax.dynamic_slice(wave_coef, (row, zero), (quarter, own_cols))

    reach = float(pairs * ops * width) * TOP * TOP

    own = [wave_coef]
    wave = wave_coef.astype(bf16)
    other = [across(wave)]
    weight = jnp.sum(wave_coef * wave_coef)
    weight = weight + across(weight)
    norm = jnp.ones((), f32)
    for step in range(STEPS):
        if step == 0:
            place = [sent, zero, core * own_cols, zero, (1 - core) * own_cols]
        else:
            place = [sent]
            for c, (b0, b1) in ((core, (bit0, bit1)), (1 - core, (there0, there1))):
                for first in quarters(b0, b1):
                    place += [first, c * own_cols]
        place = jnp.stack(place).astype(jnp.int32)
        inner, send = sigma_halves(place, mask, own, other, right, left, blocks)
        length = jnp.sqrt(weight) + 1e-30
        scale = 32768.0 / (reach * length)
        got = swap((send * scale).astype(f16), 0)
        keep, corr = sigma_kept(place, mask, own, send, inner, left, blocks)
        corr = corr.reshape(())
        corr = corr + across(corr)
        corr = corr + swap(corr, 0)
        keep = keep * scale + got.astype(f32)
        send = lax.dynamic_slice(keep, ((1 - bit1) * quarter, zero), (quarter, own_cols)).astype(f16)
        keep = lax.dynamic_slice(keep, (bit1 * quarter, zero), (quarter, own_cols))
        got = swap(send, 1)
        corr = corr + swap(corr, 1)
        keep = keep + got.astype(f32)
        for stage in range(2, stages):
            send = keep.astype(f16)
            got = swap(send, stage)
            corr = corr + swap(corr, stage)
            keep = send.astype(f32) + got.astype(f32)
        sigma = keep * (norm / scale)
        square = norm * norm
        theta = (corr * square / cells) / (weight * square / cells + EPS)
        spacing = diag - theta
        correction = (sigma - theta * coef) * spacing / jnp.maximum(spacing * spacing, 1.0)
        moved = coef - correction
        last = step == STEPS - 1
        if last:
            shrink = 32768.0 / ((1.0 + jnp.abs(theta) + reach) * (length * norm))
            moved = moved * shrink
            piece = moved.astype(f16)
        else:
            piece = moved.astype(bf16)
        weight = jnp.sum(moved * moved)
        p1 = swap(piece, 1)
        p2 = swap(piece, 0)
        weight = weight + across(weight)
        p1, weight = lax.optimization_barrier((p1, weight))
        p3 = swap(p1, 0)
        weight = weight + swap(weight, 1)
        p3, weight = lax.optimization_barrier((p3, weight))
        weight = weight + swap(weight, 0)
        if not last:
            norm = lax.rsqrt(weight / cells + EPS)
            coef = moved * norm
            own = [piece, p1, p2, p3]
            other = [across(p) for p in own]
        else:
            norm = lax.rsqrt(weight / cells + EPS * shrink * shrink)
            near0, near1 = jnp.where(bit1 == 0, piece, p1), jnp.where(bit1 == 0, p1, piece)
            far0, far1 = jnp.where(bit1 == 0, p2, p3), jnp.where(bit1 == 0, p3, p2)
            full = jnp.concatenate([
                jnp.where(bit0 == 0, near0, far0), jnp.where(bit0 == 0, near1, far1),
                jnp.where(bit0 == 0, far0, near0), jnp.where(bit0 == 0, far1, near1)], axis=0)
            return full.astype(f32) * norm


def solution(mesh):
    in_specs = (
        P("geom", "col"),
        P("geom", "col"),
        P(("geom", "op"), None, None),
        P(("geom", "op"), None, "col"),
        P(("geom", "op"), None, None),
    )
    body = functools.partial(local, mesh.shape["op"], mesh.shape["col"])
    return jax.shard_map(body, mesh=mesh, in_specs=in_specs, out_specs=P("geom", "col"), check_vma=False)
```

```python
import functools

import jax
import jax.numpy as jnp
from jax import lax
from jax.experimental import pallas as pl
from jax.experimental.pallas import tpu as pltpu
from jax.sharding import PartitionSpec as P

STEPS = 2
CHUNKS = 2
EPS = 1e-06
TOP = 0.1875
BOTH = ("op", "col")
F32, F16, BF16 = jnp.float32, jnp.float16, jnp.bfloat16
SDS = jax.ShapeDtypeStruct
ANY = pl.BlockSpec(memory_space=pl.ANY)
VMEM = pl.BlockSpec(memory_space=pltpu.VMEM)
SMEM = pl.BlockSpec(memory_space=pltpu.SMEM)
ONE = SDS((1, 1), F32)
ORDER = ((1, 2), (2, 1))


def call(kernel, name, outs, out_specs, in_specs, args, flops, moved, scratch=()):
    return pl.pallas_call(
        kernel, out_shape=outs, in_specs=in_specs, out_specs=out_specs, scratch_shapes=scratch, name=name,
        compiler_params=pltpu.CompilerParams(vmem_limit_bytes=24 * 2 ** 20),
        cost_estimate=pl.CostEstimate(flops=flops, bytes_accessed=moved, transcendentals=0))(*args)


def total(own_ref, other_ref):
    return jnp.full((1, 1), own_ref[0, 0] + other_ref[0, 0], F32)


def scale_of(reach, weight):
    return 32768.0 / (reach * (jnp.sqrt(weight) + 1e-30))


def open_vector(coef):
    rows, cols = coef.shape
    parts = 4
    step = rows // parts

    def kernel(coef_ref, full_ref, wave_ref, weight_ref, sems):
        copies = []
        for p in range(parts):
            at = pl.ds(p * step, step)
            copies.append(pltpu.make_async_copy(coef_ref.at[at], full_ref.at[at], sems.at[p]))
            copies[-1].start()
        weight = jnp.zeros((8, cols), F32)
        for p in range(parts):
            copies[p].wait()
            block = full_ref[p * step:(p + 1) * step, :]
            wave_ref[p * step:(p + 1) * step, :] = block.astype(BF16)
            weight = weight + jnp.sum((block * block).reshape(step // 8, 8, cols), axis=0)
        weight_ref[0, 0] = jnp.sum(weight)

    return call(kernel, "open_vector", (SDS((rows, cols), F32), SDS((rows, cols), BF16), ONE), (VMEM, VMEM, SMEM),
                [ANY], (coef,), 3 * rows * cols, 8 * rows * cols, [pltpu.SemaphoreType.DMA((parts,))])


def masked_halves(left, mask, blocks):
    pairs, width, _ = left.shape
    half, inside = width // 2, width // blocks

    def kernel(mask_ref, left_ref, out_ref, buf, sems):
        copies = {}
        for h in range(2):
            for k in range(pairs):
                at = (k, pl.ds(h * half, half))
                copies[h, k] = pltpu.make_async_copy(left_ref.at[at], buf.at[at], sems.at[h * pairs + k])
                copies[h, k].start()
        for h in range(2):
            for k in range(pairs):
                copies[h, k].wait()
                for i in range(half // inside):
                    for j in range(blocks):
                        keep = mask_ref[(k * blocks + h * half // inside + i) * blocks + j]
                        block = buf[k, h * half + i * inside:h * half + (i + 1) * inside, j * inside:(j + 1) * inside]
                        out_ref[h, i * inside:(i + 1) * inside, k * width + j * inside:k * width + (j + 1) * inside] = (
                            jnp.where(keep != 0, block, jnp.zeros_like(block)))

    return call(kernel, "masked_halves", SDS((2, half, pairs * width), BF16), VMEM, [SMEM, ANY], (mask, left),
                left.size, 4 * left.size,
                [pltpu.VMEM(left.shape, BF16), pltpu.SemaphoreType.DMA((2 * pairs,))])


def sent_half(chunk, reach, place, weights, own, other, right, masked):
    pairs, width, cols = right.shape
    size, half = cols // CHUNKS, width // 2
    at = slice(chunk * size, (chunk + 1) * size)

    def kernel(place_ref, a_ref, b_ref, own_ref, other_ref, right_ref, masked_ref, inner_ref, send_ref):
        scale = scale_of(reach, total(a_ref, b_ref))
        here = pl.ds(pl.multiple_of(place_ref[0], cols), cols)
        there = pl.ds(pl.multiple_of(place_ref[1], cols), cols)
        for k in range(pairs):
            inner_ref[k * width:(k + 1) * width, :] = (
                jnp.dot(own_ref[...], right_ref[k, here, at], preferred_element_type=F32)
                + jnp.dot(other_ref[...], right_ref[k, there, at], preferred_element_type=F32)).astype(BF16)
        send_ref[...] = scale * jnp.dot(masked_ref[place_ref[2]], inner_ref[...], preferred_element_type=F32)

    return call(kernel, "sent_half_%d" % chunk, (SDS((pairs * width, size), BF16), SDS((half, size), F32)),
                (VMEM, VMEM), [SMEM] * 3 + [VMEM] * 4, (place, *weights, own, other, right, masked),
                3 * pairs * width * width * size, 2 ** 20)


def kept_half(reach, place, weights, inner, masked):
    _, half, depth = masked.shape
    size = inner.shape[1]

    def kernel(place_ref, a_ref, b_ref, inner_ref, masked_ref, keep_ref):
        scale = scale_of(reach, total(a_ref, b_ref))
        keep_ref[...] = scale * jnp.dot(masked_ref[1 - place_ref[2]], inner_ref[...], preferred_element_type=F32)

    return call(kernel, "kept_half", SDS((half, size), F32), VMEM, [SMEM] * 3 + [VMEM] * 2,
                (place, *weights, inner, masked), 2 * half * depth * size, 2 ** 20)


def correlate(vector, sigmas):
    rows, cols = vector.shape
    size = cols // len(sigmas)

    def kernel(vector_ref, *refs):
        out = jnp.zeros((8, size), F32)
        for c, sigma_ref in enumerate(refs[:-1]):
            product = vector_ref[:, c * size:(c + 1) * size] * sigma_ref[...]
            out = out + jnp.sum(product.reshape(rows // 8, 8, size), axis=0)
        refs[-1][0, 0] = jnp.sum(out)

    return call(kernel, "correlate", ONE, SMEM, [VMEM] * (1 + len(sigmas)), (vector, *sigmas), 2 * rows * cols, 2 ** 20)


def correct(first, reach, cells, vector, sigmas, diag, corr, weights):
    rows, cols = vector.shape
    size = cols // len(sigmas)

    def kernel(corr_a, corr_b, weight_a, weight_b, vector_ref, diag_ref, *refs):
        sigma_refs, (moved_ref, wave_ref, square_ref) = refs[:-3], refs[-3:]
        weight = total(weight_a, weight_b)
        scale = scale_of(reach, weight)
        norm = jnp.ones((1, 1), F32) if first else lax.rsqrt(weight / cells + EPS)
        square = norm * norm
        theta = (total(corr_a, corr_b) / scale * square / cells) / (weight * square / cells + EPS)
        unit = norm / scale
        out = jnp.zeros((8, size), F32)
        for c, sigma_ref in enumerate(sigma_refs):
            at = slice(c * size, (c + 1) * size)
            coef = vector_ref[:, at] * norm
            spacing = diag_ref[:, at] - theta
            moved = coef - (sigma_ref[...] * unit - theta * coef) * spacing / jnp.maximum(spacing * spacing, 1.0)
            moved_ref[:, at] = moved
            wave_ref[:, at] = moved.astype(BF16)
            out = out + jnp.sum((moved * moved).reshape(rows // 8, 8, size), axis=0)
        square_ref[0, 0] = jnp.sum(out)

    return call(kernel, "correct", (SDS((rows, cols), F32), SDS((rows, cols), BF16), ONE), (VMEM, VMEM, SMEM),
                [SMEM] * 4 + [VMEM] * (2 + len(sigmas)), (*corr, *weights, vector, diag, *sigmas),
                12 * rows * cols, 2 ** 20)


def normalise(cells, vector, weights):
    rows, cols = vector.shape
    parts = 4
    step = rows // parts

    def kernel(weight_a, weight_b, vector_ref, out_ref, buf, sems):
        norm = lax.rsqrt(total(weight_a, weight_b) / cells + EPS)
        copies = []
        for p in range(parts):
            at = pl.ds(p * step, step)
            buf[p * step:(p + 1) * step, :] = vector_ref[p * step:(p + 1) * step, :] * norm
            copies.append(pltpu.make_async_copy(buf.at[at], out_ref.at[at], sems.at[p]))
            copies[-1].start()
        for copy in copies:
            copy.wait()

    return call(kernel, "normalise", SDS((rows, cols), F32), ANY, [SMEM] * 2 + [VMEM], (*weights, vector),
                rows * cols, 8 * rows * cols, [pltpu.VMEM((rows, cols), F32), pltpu.SemaphoreType.DMA((parts,))])


def local(ops, cols, wave_coef, diag_energy, left, right, block_mask):
    pairs, width, _ = left.shape
    own_cols = right.shape[2]
    blocks = block_mask.shape[1]
    cells = float(width * width)
    half, quarter, size = width // 2, width // 4, own_cols // CHUNKS
    stages = ops.bit_length() - 1
    reach = float(pairs * ops * width) * TOP * TOP

    def swap(x, stage):
        pairing = []
        for o in range(ops):
            for c in range(cols):
                bit = ORDER[c % 2][stage] if stage < 2 else 1 << stage
                pairing.append((o * cols + c, (o ^ bit) * cols + c))
        return lax.ppermute(x, BOTH, pairing)

    def across(x):
        return lax.ppermute(x, "col", [(c, c ^ 1) for c in range(cols)])

    me, core = lax.axis_index("op"), lax.axis_index("col")
    low, high = me % 2, (me // 2) % 2
    bit0, bit1 = jnp.where(core == 0, low, high), jnp.where(core == 0, high, low)
    zero = jnp.zeros((), jnp.int32)
    place = jnp.stack([core * own_cols, (1 - core) * own_cols, 1 - bit0]).astype(jnp.int32)

    def reduced(send, keep):
        got = swap(send.astype(F16), 0)
        keep = keep + got.astype(F32)
        send = lax.dynamic_slice(keep, ((1 - bit1) * quarter, zero), (quarter, size)).astype(F16)
        keep = lax.dynamic_slice(keep, (bit1 * quarter, zero), (quarter, size))
        keep = keep + swap(send, 1).astype(F32)
        for stage in range(2, stages):
            send = keep.astype(F16)
            keep = send.astype(F32) + swap(send, stage).astype(F32)
        return keep.astype(F16)

    def gathered(piece):
        p1, p2 = swap(piece, 1), swap(piece, 0)
        p3 = swap(p1, 0)
        near0, near1 = jnp.where(bit1 == 0, piece, p1), jnp.where(bit1 == 0, p1, piece)
        far0, far1 = jnp.where(bit1 == 0, p2, p3), jnp.where(bit1 == 0, p3, p2)
        return jnp.concatenate([
            jnp.where(bit0 == 0, near0, far0), jnp.where(bit0 == 0, near1, far1),
            jnp.where(bit0 == 0, far0, near0), jnp.where(bit0 == 0, far1, near1)], axis=0).astype(F32)

    vector, own, weight = open_vector(wave_coef)
    masked = masked_halves(left, block_mask.reshape(-1), blocks)
    for step in range(STEPS):
        other = across(own)
        weights = (weight, across(weight))
        parts = [sent_half(c, reach, place, weights, own, other, right, masked) for c in range(CHUNKS)]
        sigmas = [gathered(reduced(send, kept_half(reach, place, weights, inner, masked))) for inner, send in parts]
        corr = correlate(vector, sigmas)
        vector, own, weight = correct(
            step == 0, reach, cells, vector, sigmas, diag_energy, (corr, across(corr)), weights)
    return normalise(cells, vector, (weight, across(weight)))


def solution(mesh):
    in_specs = (
        P("geom", "col"),
        P("geom", "col"),
        P(("geom", "op"), None, None),
        P(("geom", "op"), None, "col"),
        P(("geom", "op"), None, None),
    )
    body = functools.partial(local, mesh.shape["op"], mesh.shape["col"])
    return jax.shard_map(body, mesh=mesh, in_specs=in_specs, out_specs=P("geom", "col"), check_vma=False)
```

```python
import functools

import jax
import jax.numpy as jnp
from jax import lax
from jax.experimental import pallas as pl
from jax.experimental.pallas import tpu as pltpu
from jax.sharding import PartitionSpec as P

STEPS = 2
CHUNKS = 2
EPS = 1e-06
BLOCK = 16
TOP = 0.1875
BOTH = ("op", "col")
F32, F16, BF16 = jnp.float32, jnp.float16, jnp.bfloat16
SDS = jax.ShapeDtypeStruct
ANY = pl.BlockSpec(memory_space=pl.ANY)
VMEM = pl.BlockSpec(memory_space=pltpu.VMEM)
SMEM = pl.BlockSpec(memory_space=pltpu.SMEM)
ONE = SDS((8, 128), F32)
ORDER = ((1, 2), (2, 1))


def call(kernel, name, outs, out_specs, in_specs, args, flops, moved, scratch=(), mib=8):
    return pl.pallas_call(
        kernel, out_shape=outs, in_specs=in_specs, out_specs=out_specs, scratch_shapes=scratch, name=name,
        compiler_params=pltpu.CompilerParams(vmem_limit_bytes=mib * 2 ** 20),
        cost_estimate=pl.CostEstimate(flops=flops, bytes_accessed=moved, transcendentals=0))(*args)


def total(own_ref, other_ref):
    return own_ref[:1, :1] + other_ref[:1, :1]


def put(ref, parts):
    ref[...] = jnp.full(ref.shape, jnp.sum(parts), F32)


def folded(block):
    return jnp.sum(block.reshape(block.shape[0] // 8, 8, block.shape[1]), axis=0)


def scale_of(reach, weight):
    return 32768.0 / (reach * (jnp.sqrt(weight) + 1e-30))


def open_vector(coef):
    rows, cols = coef.shape
    parts = 4
    step = rows // parts

    def kernel(coef_ref, full_ref, wave_ref, weight_ref, sems):
        copies = []
        for p in range(parts):
            at = pl.ds(p * step, step)
            copies.append(pltpu.make_async_copy(coef_ref.at[at], full_ref.at[at], sems.at[p]))
            copies[-1].start()
        weight = jnp.zeros((8, cols), F32)
        for p in range(parts):
            copies[p].wait()
            for r in range(p * step, (p + 1) * step, BLOCK):
                block = full_ref[r:r + BLOCK, :]
                wave_ref[r:r + BLOCK, :] = block.astype(BF16)
                weight = weight + folded(block * block)
        put(weight_ref, weight)

    return call(kernel, "open_vector", (SDS((rows, cols), F32), SDS((rows, cols), BF16), ONE), (VMEM, VMEM, VMEM),
                [ANY], (coef,), 3 * rows * cols, 8 * rows * cols, [pltpu.SemaphoreType.DMA((parts,))])


def first_half():
    me, core = lax.axis_index("op"), lax.axis_index("col")
    bit = 0
    for c, (mask, _) in enumerate(ORDER):
        bit = bit + jnp.where(core == c, (me // mask) % 2, 0)
    return 1 - bit


def masked_half(left, mask, blocks, sent):
    pairs, width, _ = left.shape
    half, inside = width // 2, width // blocks

    def kernel(mask_ref, left_ref, out_ref, buf, sems):
        h = first_half() if sent else 1 - first_half()
        copies = []
        for k in range(pairs):
            copies.append(pltpu.make_async_copy(
                left_ref.at[k, pl.ds(pl.multiple_of(h * half, half), half)], buf.at[k], sems.at[k]))
            copies[-1].start()
        for k in range(pairs):
            copies[k].wait()
            for i in range(half // inside):
                for j in range(blocks):
                    keep = mask_ref[(k * blocks + h * (half // inside) + i) * blocks + j]
                    block = buf[k, i * inside:(i + 1) * inside, j * inside:(j + 1) * inside]
                    out_ref[i * inside:(i + 1) * inside, k * width + j * inside:k * width + (j + 1) * inside] = (
                        jnp.where(keep != 0, block, jnp.zeros_like(block)))

    return call(kernel, "masked_sent" if sent else "masked_kept", SDS((half, pairs * width), BF16), VMEM,
                [SMEM, ANY], (mask, left), left.size, 2 * left.size,
                [pltpu.VMEM((pairs, half, width), BF16), pltpu.SemaphoreType.DMA((pairs,))])


def product(out_ref, at, scale, left_ref, right_ref, parts=4):
    step = left_ref.shape[0] // parts
    for p in range(parts):
        rows = slice(p * step, (p + 1) * step)
        out_ref[rows, at] = scale * jnp.dot(left_ref[rows, :], right_ref[...], preferred_element_type=F32)


def sent_half(chunk, reach, weights, own, other, right, masked):
    pairs, width, cols = right.shape
    size, half = cols // CHUNKS, width // 2
    at = slice(chunk * size, (chunk + 1) * size)
    step = width // 4

    def kernel(a_ref, b_ref, own_ref, other_ref, right_ref, masked_ref, inner_ref, send_ref):
        core = lax.axis_index("col")
        here = pl.ds(pl.multiple_of(core * cols, cols), cols)
        there = pl.ds(pl.multiple_of((1 - core) * cols, cols), cols)
        scale = scale_of(reach, total(a_ref, b_ref))
        for k in range(pairs):
            near, far = right_ref[k, here, at], right_ref[k, there, at]
            for r in range(0, width, step):
                inner_ref[k * width + r:k * width + r + step, :] = (
                    jnp.dot(own_ref[r:r + step, :], near, preferred_element_type=F32)
                    + jnp.dot(other_ref[r:r + step, :], far, preferred_element_type=F32)).astype(BF16)
        product(send_ref, slice(None), scale, masked_ref, inner_ref, 2)

    return call(kernel, "sent_half_%d" % chunk, (SDS((pairs * width, size), BF16), SDS((half, size), F32)),
                (VMEM, VMEM), [VMEM] * 6, (*weights, own, other, right, masked),
                3 * pairs * width * width * size, 2 ** 20)


def kept_half(reach, weights, inner, masked):
    half, depth = masked.shape
    size = inner.shape[1]

    def kernel(a_ref, b_ref, inner_ref, masked_ref, keep_ref):
        product(keep_ref, slice(None), scale_of(reach, total(a_ref, b_ref)), masked_ref, inner_ref, 2)

    return call(kernel, "kept_half", SDS((half, size), F32), VMEM, [VMEM] * 4,
                (*weights, inner, masked), 2 * half * depth * size, 2 ** 20)


def correlate(vector, sigmas):
    rows, cols = vector.shape
    size = cols // len(sigmas)

    def kernel(vector_ref, *refs):
        out = jnp.zeros((8, size), F32)
        for r in range(0, rows, BLOCK):
            for c, sigma_ref in enumerate(refs[:-1]):
                out = out + folded(vector_ref[r:r + BLOCK, c * size:(c + 1) * size] * sigma_ref[r:r + BLOCK, :])
        put(refs[-1], out)

    return call(kernel, "correlate", ONE, VMEM, [VMEM] * (1 + len(sigmas)), (vector, *sigmas), 2 * rows * cols, 2 ** 20)


def correct(first, reach, cells, vector, sigmas, diag, corr, weights):
    rows, cols = vector.shape
    size = cols // len(sigmas)

    def kernel(corr_a, corr_b, weight_a, weight_b, vector_ref, diag_ref, *refs):
        sigma_refs, (moved_ref, wave_ref, square_ref) = refs[:-3], refs[-3:]
        weight = total(weight_a, weight_b)
        scale = scale_of(reach, weight)
        norm = jnp.ones((1, 1), F32) if first else lax.rsqrt(weight / cells + EPS)
        square = norm * norm
        theta = (total(corr_a, corr_b) / scale * square / cells) / (weight * square / cells + EPS)
        unit = norm / scale
        out = jnp.zeros((8, size), F32)
        for r in range(0, rows, BLOCK):
            for c, sigma_ref in enumerate(sigma_refs):
                at = (slice(r, r + BLOCK), slice(c * size, (c + 1) * size))
                coef = vector_ref[at] * norm
                spacing = diag_ref[at] - theta
                slope = spacing / jnp.maximum(spacing * spacing, 1.0)
                moved = coef - (sigma_ref[r:r + BLOCK, :] * unit - theta * coef) * slope
                moved_ref[at] = moved
                wave_ref[at] = moved.astype(BF16)
                out = out + folded(moved * moved)
        put(square_ref, out)

    return call(kernel, "correct", (SDS((rows, cols), F32), SDS((rows, cols), BF16), ONE), (VMEM, VMEM, VMEM),
                [VMEM] * (6 + len(sigmas)), (*corr, *weights, vector, diag, *sigmas), 12 * rows * cols, 2 ** 20)


def normalise(cells, vector, weights):
    rows, cols = vector.shape
    parts = 4
    step = rows // parts

    def kernel(weight_a, weight_b, vector_ref, out_ref, buf, sems):
        norm = lax.rsqrt(total(weight_a, weight_b) / cells + EPS)
        copies = []
        for p in range(parts):
            at = pl.ds(p * step, step)
            for r in range(p * step, (p + 1) * step, BLOCK):
                buf[r:r + BLOCK, :] = vector_ref[r:r + BLOCK, :] * norm
            copies.append(pltpu.make_async_copy(buf.at[at], out_ref.at[at], sems.at[p]))
            copies[-1].start()
        for copy in copies:
            copy.wait()

    return call(kernel, "normalise", SDS((rows, cols), F32), ANY, [VMEM] * 3, (*weights, vector),
                rows * cols, 8 * rows * cols, [pltpu.VMEM((rows, cols), F32), pltpu.SemaphoreType.DMA((parts,))])


def local(ops, cols, wave_coef, diag_energy, left, right, block_mask):
    pairs, width, _ = left.shape
    own_cols = right.shape[2]
    blocks = block_mask.shape[1]
    cells = float(width * width)
    half, quarter, size = width // 2, width // 4, own_cols // CHUNKS
    stages = ops.bit_length() - 1
    reach = float(pairs * ops * width) * TOP * TOP

    def swap(x, stage):
        pairing = []
        for o in range(ops):
            for c in range(cols):
                bit = ORDER[c % 2][stage] if stage < 2 else 1 << stage
                pairing.append((o * cols + c, (o ^ bit) * cols + c))
        return lax.ppermute(x, BOTH, pairing)

    def across(x):
        return lax.ppermute(x, "col", [(c, c ^ 1) for c in range(cols)])

    me, core = lax.axis_index("op"), lax.axis_index("col")
    low, high = me % 2, (me // 2) % 2
    bit0, bit1 = jnp.where(core == 0, low, high), jnp.where(core == 0, high, low)
    zero = jnp.zeros((), jnp.int32)

    def begin(send):
        return swap(send.astype(F16), 0)

    def halve(keep, got):
        keep = keep + got.astype(F32)
        send = lax.dynamic_slice(keep, ((1 - bit1) * quarter, zero), (quarter, size)).astype(F16)
        return send, lax.dynamic_slice(keep, (bit1 * quarter, zero), (quarter, size))

    def finish(keep, got):
        keep = keep + got.astype(F32)
        for stage in range(2, stages):
            send = keep.astype(F16)
            keep = send.astype(F32) + swap(send, stage).astype(F32)
        return keep.astype(F16)

    def gathered(piece):
        p1, p2 = swap(piece, 1), swap(piece, 0)
        p3 = swap(p1, 0)
        near0, near1 = jnp.where(bit1 == 0, piece, p1), jnp.where(bit1 == 0, p1, piece)
        far0, far1 = jnp.where(bit1 == 0, p2, p3), jnp.where(bit1 == 0, p3, p2)
        return jnp.concatenate([
            jnp.where(bit0 == 0, near0, far0), jnp.where(bit0 == 0, near1, far1),
            jnp.where(bit0 == 0, far0, near0), jnp.where(bit0 == 0, far1, near1)], axis=0).astype(F32)

    vector, own, weight = open_vector(wave_coef)
    mask = block_mask.reshape(-1)
    sent, kept = masked_half(left, mask, blocks, True), masked_half(left, mask, blocks, False)
    for step in range(STEPS):
        other = across(own)
        weights = (weight, across(weight))
        inners, keeps, gots = [], [], []
        for c in range(CHUNKS):
            inner, send = sent_half(c, reach, weights, own, other, right, sent)
            gots.append(begin(send))
            inners.append(inner)
            own, other = lax.optimization_barrier((own, other, inner))[:2]
        inners[0] = lax.optimization_barrier((inners[0], inners[-1]))[0]
        sigmas = []
        for c in range(CHUNKS):
            keep = kept_half(reach, weights, inners[c], kept)
            send, keep = halve(keep, gots[c])
            if c + 1 < CHUNKS:
                send, inners[c + 1] = lax.optimization_barrier((send, inners[c + 1]))
            sigmas.append(gathered(finish(keep, swap(send, 1))))
        corr = correlate(vector, sigmas)
        vector, own, weight = correct(
            step == 0, reach, cells, vector, sigmas, diag_energy, (corr, across(corr)), weights)
    return normalise(cells, vector, (weight, across(weight)))


def solution(mesh):
    in_specs = (
        P("geom", "col"),
        P("geom", "col"),
        P(("geom", "op"), None, None),
        P(("geom", "op"), None, "col"),
        P(("geom", "op"), None, None),
    )
    body = functools.partial(local, mesh.shape["op"], mesh.shape["col"])
    return jax.shard_map(body, mesh=mesh, in_specs=in_specs, out_specs=P("geom", "col"), check_vma=False)
```

```python
import functools

import jax
import jax.numpy as jnp
from jax import lax
from jax.experimental import pallas as pl
from jax.experimental.pallas import tpu as pltpu
from jax.sharding import PartitionSpec as P

STEPS = 2
CHUNKS = 2
EPS = 1e-06
BLOCK = 16
TOP = 0.1875
BOTH = ("op", "col")
F32, F16, BF16 = jnp.float32, jnp.float16, jnp.bfloat16
SDS = jax.ShapeDtypeStruct
ANY = pl.BlockSpec(memory_space=pl.ANY)
VMEM = pl.BlockSpec(memory_space=pltpu.VMEM)
SMEM = pl.BlockSpec(memory_space=pltpu.SMEM)
ONE = SDS((8, 128), F32)
ORDER = ((1, 2), (2, 1))


def in_hbm(x):
    return pltpu.with_memory_space_constraint(x, pltpu.HBM)


def call(kernel, name, outs, out_specs, in_specs, args, flops, moved, scratch=(), mib=8):
    return pl.pallas_call(
        kernel, out_shape=outs, in_specs=in_specs, out_specs=out_specs, scratch_shapes=scratch, name=name,
        compiler_params=pltpu.CompilerParams(vmem_limit_bytes=mib * 2 ** 20),
        cost_estimate=pl.CostEstimate(flops=flops, bytes_accessed=moved, transcendentals=0))(*args)


def total(own_ref, other_ref):
    return own_ref[:1, :1] + other_ref[:1, :1]


def put(ref, parts):
    ref[...] = jnp.full(ref.shape, jnp.sum(parts), F32)


def folded(block):
    return jnp.sum(block.reshape(block.shape[0] // 8, 8, block.shape[1]), axis=0)


def scale_of(reach, weight):
    return 32768.0 / (reach * (jnp.sqrt(weight) + 1e-30))


def open_vector(coef):
    rows, cols = coef.shape
    parts = 4
    step = rows // parts

    def kernel(coef_ref, wave_ref, weight_ref, buf, sems):
        copies = []
        for p in range(parts):
            at = pl.ds(p * step, step)
            copies.append(pltpu.make_async_copy(coef_ref.at[at], buf.at[at], sems.at[p]))
            copies[-1].start()
        weight = jnp.zeros((8, cols), F32)
        for p in range(parts):
            copies[p].wait()
            for r in range(p * step, (p + 1) * step, BLOCK):
                block = buf[r:r + BLOCK, :]
                wave_ref[r:r + BLOCK, :] = block.astype(BF16)
                weight = weight + folded(block * block)
        put(weight_ref, weight)

    return call(kernel, "open_vector", (SDS((rows, cols), BF16), ONE), (VMEM, VMEM), [ANY], (in_hbm(coef),),
                3 * rows * cols, 8 * rows * cols,
                [pltpu.VMEM((rows, cols), F32), pltpu.SemaphoreType.DMA((parts,))], mib=12)


def first_half():
    me, core = lax.axis_index("op"), lax.axis_index("col")
    bit = 0
    for c, (mask, _) in enumerate(ORDER):
        bit = bit + jnp.where(core == c, (me // mask) % 2, 0)
    return 1 - bit


def operators(left, right, mask, blocks):
    pairs, width, _ = left.shape
    half, inside = width // 2, width // blocks
    strips = half // inside

    def kernel(mask_ref, left_ref, right_ref, sent_ref, kept_ref, held_ref, buf, sems, right_sems):
        first = first_half()
        order = [(o, k, i) for o in range(2) for k in range(pairs) for i in range(strips)]
        copies, rights = [], []
        for k in range(pairs):
            rights.append(pltpu.make_async_copy(right_ref.at[k], held_ref.at[k], right_sems.at[k]))
        for n, (o, k, i) in enumerate(order):
            h = first if o == 0 else 1 - first
            copies.append(pltpu.make_async_copy(
                left_ref.at[k, pl.ds(pl.multiple_of(h * half + i * inside, inside), inside)], buf.at[n], sems.at[n]))
        for copy in copies + rights:
            copy.start()
        for n, (o, k, i) in enumerate(order):
            h, out_ref = (first, sent_ref) if o == 0 else (1 - first, kept_ref)
            copies[n].wait()
            for j in range(blocks):
                keep = mask_ref[(k * blocks + h * strips + i) * blocks + j]
                block = buf[n, :, j * inside:(j + 1) * inside]
                out_ref[i * inside:(i + 1) * inside, k * width + j * inside:k * width + (j + 1) * inside] = (
                    jnp.where(keep != 0, block, jnp.zeros_like(block)))
        for copy in rights:
            copy.wait()

    count = 2 * pairs * strips
    half_out = SDS((half, pairs * width), BF16)
    return call(kernel, "operators", (half_out, half_out, SDS(right.shape, BF16)), (VMEM,) * 3, [SMEM, ANY, ANY],
                (mask, in_hbm(left), in_hbm(right)), left.size, 4 * left.size,
                [pltpu.VMEM((count, inside, width), BF16), pltpu.SemaphoreType.DMA((count,)),
                 pltpu.SemaphoreType.DMA((pairs,))], mib=12)


def product(out_ref, at, scale, left_ref, right_ref, parts=4):
    step = left_ref.shape[0] // parts
    for p in range(parts):
        rows = slice(p * step, (p + 1) * step)
        out_ref[rows, at] = scale * jnp.dot(left_ref[rows, :], right_ref[...], preferred_element_type=F32)


def sent_half(chunk, reach, weights, own, other, right, masked):
    pairs, width, cols = right.shape
    size, half = cols // CHUNKS, width // 2
    at = slice(chunk * size, (chunk + 1) * size)
    step = width // 4

    def kernel(a_ref, b_ref, own_ref, other_ref, right_ref, masked_ref, inner_ref, send_ref):
        core = lax.axis_index("col")
        here = pl.ds(pl.multiple_of(core * cols, cols), cols)
        there = pl.ds(pl.multiple_of((1 - core) * cols, cols), cols)
        scale = scale_of(reach, total(a_ref, b_ref))
        for k in range(pairs):
            near, far = right_ref[k, here, at], right_ref[k, there, at]
            for r in range(0, width, step):
                inner_ref[k * width + r:k * width + r + step, :] = (
                    jnp.dot(own_ref[r:r + step, :], near, preferred_element_type=F32)
                    + jnp.dot(other_ref[r:r + step, :], far, preferred_element_type=F32)).astype(BF16)
        product(send_ref, slice(None), scale, masked_ref, inner_ref, 2)

    return call(kernel, "sent_half_%d" % chunk, (SDS((pairs * width, size), BF16), SDS((half, size), F32)),
                (VMEM, VMEM), [VMEM] * 6, (*weights, own, other, right, masked),
                3 * pairs * width * width * size, 2 ** 20)


def kept_half(reach, weights, inner, masked):
    half, depth = masked.shape
    size = inner.shape[1]

    def kernel(a_ref, b_ref, inner_ref, masked_ref, keep_ref):
        product(keep_ref, slice(None), scale_of(reach, total(a_ref, b_ref)), masked_ref, inner_ref, 2)

    return call(kernel, "kept_half", SDS((half, size), F32), VMEM, [VMEM] * 4,
                (*weights, inner, masked), 2 * half * depth * size, 2 ** 20)


def correlate(vector, sigmas):
    rows, cols = vector.shape
    size = cols // len(sigmas)

    def kernel(vector_ref, *refs):
        out = jnp.zeros((8, size), F32)
        for r in range(0, rows, BLOCK):
            for c, sigma_ref in enumerate(refs[:-1]):
                out = out + folded(vector_ref[r:r + BLOCK, c * size:(c + 1) * size] * sigma_ref[r:r + BLOCK, :])
        put(refs[-1], out)

    return call(kernel, "correlate", ONE, VMEM, [VMEM] * (1 + len(sigmas)), (vector, *sigmas), 2 * rows * cols, 2 ** 20)


def correct(first, reach, cells, vector, sigmas, diag, corr, weights):
    rows, cols = vector.shape
    size = cols // len(sigmas)

    def kernel(corr_a, corr_b, weight_a, weight_b, vector_ref, diag_ref, *refs):
        sigma_refs, (moved_ref, wave_ref, square_ref) = refs[:-3], refs[-3:]
        weight = total(weight_a, weight_b)
        scale = scale_of(reach, weight)
        norm = jnp.ones((1, 1), F32) if first else lax.rsqrt(weight / cells + EPS)
        square = norm * norm
        theta = (total(corr_a, corr_b) / scale * square / cells) / (weight * square / cells + EPS)
        unit = norm / scale
        out = jnp.zeros((8, size), F32)
        for r in range(0, rows, BLOCK):
            for c, sigma_ref in enumerate(sigma_refs):
                at = (slice(r, r + BLOCK), slice(c * size, (c + 1) * size))
                coef = vector_ref[at] * norm
                spacing = diag_ref[at] - theta
                slope = spacing / jnp.maximum(spacing * spacing, 1.0)
                moved = coef - (sigma_ref[r:r + BLOCK, :] * unit - theta * coef) * slope
                moved_ref[at] = moved
                wave_ref[at] = moved.astype(BF16)
                out = out + folded(moved * moved)
        put(square_ref, out)

    return call(kernel, "correct", (SDS((rows, cols), F32), SDS((rows, cols), BF16), ONE), (VMEM, VMEM, VMEM),
                [VMEM] * (6 + len(sigmas)), (*corr, *weights, vector, diag, *sigmas), 12 * rows * cols, 2 ** 20)


def normalise(cells, vector, weights):
    rows, cols = vector.shape
    parts = 4
    step = rows // parts

    def kernel(weight_a, weight_b, vector_ref, out_ref, buf, sems):
        norm = lax.rsqrt(total(weight_a, weight_b) / cells + EPS)
        copies = []
        for p in range(parts):
            at = pl.ds(p * step, step)
            for r in range(p * step, (p + 1) * step, BLOCK):
                buf[r:r + BLOCK, :] = vector_ref[r:r + BLOCK, :] * norm
            copies.append(pltpu.make_async_copy(buf.at[at], out_ref.at[at], sems.at[p]))
            copies[-1].start()
        for copy in copies:
            copy.wait()

    return call(kernel, "normalise", SDS((rows, cols), F32), ANY, [VMEM] * 3, (*weights, vector),
                rows * cols, 8 * rows * cols, [pltpu.VMEM((rows, cols), F32), pltpu.SemaphoreType.DMA((parts,))])


def local(ops, cols, wave_coef, diag_energy, left, right, block_mask):
    pairs, width, _ = left.shape
    own_cols = right.shape[2]
    blocks = block_mask.shape[1]
    cells = float(width * width)
    half, quarter, size = width // 2, width // 4, own_cols // CHUNKS
    stages = ops.bit_length() - 1
    reach = float(pairs * ops * width) * TOP * TOP

    def swap(x, stage):
        pairing = []
        for o in range(ops):
            for c in range(cols):
                bit = ORDER[c % 2][stage] if stage < 2 else 1 << stage
                pairing.append((o * cols + c, (o ^ bit) * cols + c))
        return lax.ppermute(x, BOTH, pairing)

    def across(x):
        return lax.ppermute(x, "col", [(c, c ^ 1) for c in range(cols)])

    me, core = lax.axis_index("op").astype(jnp.uint32), lax.axis_index("col").astype(jnp.uint32)
    low, high = me & 1, (me >> 1) & 1
    bit0, bit1 = jnp.where(core == 0, low, high), jnp.where(core == 0, high, low)
    low_near, low_half, zero = bit1 == 0, bit0 == 0, jnp.zeros((), jnp.uint32)
    keep_at, send_at = bit1 * quarter, (1 - bit1) * quarter
    wave_coef, keep_at, send_at, low_near, low_half = lax.optimization_barrier(
        (wave_coef, keep_at, send_at, low_near, low_half))

    def begin(send):
        return swap(send.astype(F16), 0)

    def halve(keep, got):
        keep = keep + got.astype(F32)
        send = lax.dynamic_slice(keep, (send_at, zero), (quarter, size)).astype(F16)
        return send, lax.dynamic_slice(keep, (keep_at, zero), (quarter, size))

    def finish(keep, got):
        keep = keep + got.astype(F32)
        for stage in range(2, stages):
            send = keep.astype(F16)
            keep = send.astype(F32) + swap(send, stage).astype(F32)
        return keep.astype(F16)

    def gathered(piece):
        p1, p2 = swap(piece, 1), swap(piece, 0)
        p3 = swap(p1, 0)
        near0, near1 = jnp.where(low_near, piece, p1), jnp.where(low_near, p1, piece)
        far0, far1 = jnp.where(low_near, p2, p3), jnp.where(low_near, p3, p2)
        return jnp.concatenate([
            jnp.where(low_half, near0, far0), jnp.where(low_half, near1, far1),
            jnp.where(low_half, far0, near0), jnp.where(low_half, far1, near1)], axis=0).astype(F32)

    vector = wave_coef
    own, weight = open_vector(wave_coef)
    mask = block_mask.reshape(-1)
    sent, kept, right = operators(left, right, mask, blocks)
    for step in range(STEPS):
        other = across(own)
        weights = (weight, across(weight))
        inners, keeps, gots = [], [], []
        for c in range(CHUNKS):
            inner, send = sent_half(c, reach, weights, own, other, right, sent)
            gots.append(begin(send))
            inners.append(inner)
            own, other = lax.optimization_barrier((own, other, inner))[:2]
        inners[0] = lax.optimization_barrier((inners[0], inners[-1]))[0]
        sigmas = []
        for c in range(CHUNKS):
            keep = kept_half(reach, weights, inners[c], kept)
            send, keep = halve(keep, gots[c])
            if c + 1 < CHUNKS:
                send, inners[c + 1] = lax.optimization_barrier((send, inners[c + 1]))
            sigmas.append(gathered(finish(keep, swap(send, 1))))
        corr = correlate(vector, sigmas)
        vector, own, weight = correct(
            step == 0, reach, cells, vector, sigmas, diag_energy, (corr, across(corr)), weights)
    return normalise(cells, vector, (weight, across(weight)))


def solution(mesh):
    in_specs = (
        P("geom", "col"),
        P("geom", "col"),
        P(("geom", "op"), None, None),
        P(("geom", "op"), None, "col"),
        P(("geom", "op"), None, None),
    )
    body = functools.partial(local, mesh.shape["op"], mesh.shape["col"])
    return jax.shard_map(body, mesh=mesh, in_specs=in_specs, out_specs=P("geom", "col"), check_vma=False)
```

```python
import functools

import jax
import jax.numpy as jnp
from jax import lax
from jax.experimental import pallas as pl
from jax.experimental.pallas import tpu as pltpu
from jax.sharding import PartitionSpec as P

STEPS = 2
CHUNKS = 2
EPS = 1e-06
BLOCK = 16
TOP = 0.1875
BOTH = ("op", "col")
F32, F16, BF16 = jnp.float32, jnp.float16, jnp.bfloat16
SDS = jax.ShapeDtypeStruct
ANY = pl.BlockSpec(memory_space=pl.ANY)
VMEM = pl.BlockSpec(memory_space=pltpu.VMEM)
SMEM = pl.BlockSpec(memory_space=pltpu.SMEM)
ONE = SDS((8, 128), F32)
ORDER = ((1, 2), (2, 1))


def in_hbm(x):
    return pltpu.with_memory_space_constraint(x, pltpu.HBM)


def call(kernel, name, outs, out_specs, in_specs, args, flops, moved, scratch=(), mib=8):
    return pl.pallas_call(
        kernel, out_shape=outs, in_specs=in_specs, out_specs=out_specs, scratch_shapes=scratch, name=name,
        compiler_params=pltpu.CompilerParams(vmem_limit_bytes=mib * 2 ** 20),
        cost_estimate=pl.CostEstimate(flops=flops, bytes_accessed=moved, transcendentals=0))(*args)


def total(own_ref, other_ref):
    return own_ref[:1, :1] + other_ref[:1, :1]


def put(ref, parts):
    ref[...] = jnp.full(ref.shape, jnp.sum(parts), F32)


def folded(block):
    return jnp.sum(block.reshape(block.shape[0] // 8, 8, block.shape[1]), axis=0)


def scale_of(reach, weight):
    return 32768.0 / (reach * (jnp.sqrt(weight) + 1e-30))


def open_vector(coef):
    rows, cols = coef.shape
    parts = 4
    step = rows // parts

    def kernel(coef_ref, wave_ref, weight_ref, buf, sems):
        copies = []
        for p in range(parts):
            at = pl.ds(p * step, step)
            copies.append(pltpu.make_async_copy(coef_ref.at[at], buf.at[at], sems.at[p]))
            copies[-1].start()
        weight = jnp.zeros((8, cols), F32)
        for p in range(parts):
            copies[p].wait()
            for r in range(p * step, (p + 1) * step, BLOCK):
                block = buf[r:r + BLOCK, :]
                wave_ref[r:r + BLOCK, :] = block.astype(BF16)
                weight = weight + folded(block * block)
        put(weight_ref, weight)

    return call(kernel, "open_vector", (SDS((rows, cols), BF16), ONE), (VMEM, VMEM), [ANY], (in_hbm(coef),),
                3 * rows * cols, 8 * rows * cols,
                [pltpu.VMEM((rows, cols), F32), pltpu.SemaphoreType.DMA((parts,))], mib=12)


def first_half():
    me, core = lax.axis_index("op"), lax.axis_index("col")
    bit = 0
    for c, (mask, _) in enumerate(ORDER):
        bit = bit + jnp.where(core == c, (me // mask) % 2, 0)
    return 1 - bit


def operators(left, right, mask, blocks, sent):
    pairs, width, _ = left.shape
    half, inside = width // 2, width // blocks
    strips = half // inside

    def kernel(mask_ref, left_ref, *refs):
        if sent:
            right_ref, out_ref, held_ref, buf, sems, right_sems = refs
        else:
            out_ref, buf, sems = refs
        h = first_half() if sent else 1 - first_half()
        order = [(k, i) for k in range(pairs) for i in range(strips)]
        copies = []
        for n, (k, i) in enumerate(order):
            copies.append(pltpu.make_async_copy(
                left_ref.at[k, pl.ds(pl.multiple_of(h * half + i * inside, inside), inside)], buf.at[n], sems.at[n]))
        rights = [pltpu.make_async_copy(right_ref.at[k], held_ref.at[k], right_sems.at[k])
                  for k in range(pairs)] if sent else []
        for copy in copies + rights:
            copy.start()
        for n, (k, i) in enumerate(order):
            copies[n].wait()
            for j in range(blocks):
                keep = mask_ref[(k * blocks + h * strips + i) * blocks + j]
                block = buf[n, :, j * inside:(j + 1) * inside]
                out_ref[i * inside:(i + 1) * inside, k * width + j * inside:k * width + (j + 1) * inside] = (
                    jnp.where(keep != 0, block, jnp.zeros_like(block)))
        for copy in rights:
            copy.wait()

    count = pairs * strips
    out, args = SDS((half, pairs * width), BF16), (mask, in_hbm(left))
    scratch = [pltpu.VMEM((count, inside, width), BF16), pltpu.SemaphoreType.DMA((count,))]
    if sent:
        return call(kernel, "sent_operators", (out, SDS(right.shape, BF16)), (VMEM, VMEM), [SMEM, ANY, ANY],
                    args + (in_hbm(right),), left.size, 4 * left.size,
                    scratch + [pltpu.SemaphoreType.DMA((pairs,))], mib=12)
    return call(kernel, "kept_operators", out, VMEM, [SMEM, ANY], args, left.size, 2 * left.size, scratch, mib=12)


def product(out_ref, scale, left_ref, right_ref, parts):
    step = left_ref.shape[0] // parts
    for p in range(parts):
        rows = slice(p * step, (p + 1) * step)
        out_ref[rows, :] = scale * jnp.dot(left_ref[rows, :], right_ref[...], preferred_element_type=F32)


def sent_half(chunk, reach, weights, own, other, right, masked):
    pairs, width, cols = right.shape
    size, half = cols // CHUNKS, width // 2
    at = slice(chunk * size, (chunk + 1) * size)
    step = width // 4

    def kernel(a_ref, b_ref, own_ref, other_ref, right_ref, masked_ref, inner_ref, send_ref):
        core = lax.axis_index("col")
        here = pl.ds(pl.multiple_of(core * cols, cols), cols)
        there = pl.ds(pl.multiple_of((1 - core) * cols, cols), cols)
        scale = scale_of(reach, total(a_ref, b_ref))
        for k in range(pairs):
            near, far = right_ref[k, here, at], right_ref[k, there, at]
            for r in range(0, width, step):
                inner_ref[k * width + r:k * width + r + step, :] = (
                    jnp.dot(own_ref[r:r + step, :], near, preferred_element_type=F32)
                    + jnp.dot(other_ref[r:r + step, :], far, preferred_element_type=F32)).astype(BF16)
        product(send_ref, scale, masked_ref, inner_ref, 2)

    return call(kernel, "sent_half_%d" % chunk, (SDS((pairs * width, size), BF16), SDS((half, size), F32)),
                (VMEM, VMEM), [VMEM] * 6, (*weights, own, other, right, masked),
                3 * pairs * width * width * size, 2 ** 20)


def kept_half(reach, weights, inner, masked):
    half, depth = masked.shape
    size = inner.shape[1]

    def kernel(a_ref, b_ref, inner_ref, masked_ref, keep_ref):
        product(keep_ref, scale_of(reach, total(a_ref, b_ref)), masked_ref, inner_ref, 2)

    return call(kernel, "kept_half", SDS((half, size), F32), VMEM, [VMEM] * 4,
                (*weights, inner, masked), 2 * half * depth * size, 2 ** 20)


def correlate(vector, sigmas):
    rows, cols = vector.shape
    size = cols // len(sigmas)

    def kernel(vector_ref, *refs):
        out = jnp.zeros((8, size), F32)
        for r in range(0, rows, BLOCK):
            for c, sigma_ref in enumerate(refs[:-1]):
                out = out + folded(vector_ref[r:r + BLOCK, c * size:(c + 1) * size] * sigma_ref[r:r + BLOCK, :])
        put(refs[-1], out)

    return call(kernel, "correlate", ONE, VMEM, [VMEM] * (1 + len(sigmas)), (vector, *sigmas), 2 * rows * cols, 2 ** 20)


def correct(first, last, reach, cells, vector, sigmas, diag, corr, weights):
    rows, cols = vector.shape
    size = cols // len(sigmas)

    def kernel(corr_a, corr_b, weight_a, weight_b, vector_ref, diag_ref, *refs):
        sigma_refs, (moved_ref, square_ref) = refs[:len(sigmas)], refs[len(sigmas):len(sigmas) + 2]
        weight = total(weight_a, weight_b)
        scale = scale_of(reach, weight)
        norm = jnp.ones((1, 1), F32) if first else lax.rsqrt(weight / cells + EPS)
        square = norm * norm
        theta = (total(corr_a, corr_b) / scale * square / cells) / (weight * square / cells + EPS)
        unit = norm / scale
        out = jnp.zeros((8, size), F32)
        for r in range(0, rows, BLOCK):
            for c, sigma_ref in enumerate(sigma_refs):
                at = (slice(r, r + BLOCK), slice(c * size, (c + 1) * size))
                coef = vector_ref[at] * norm
                spacing = diag_ref[at] - theta
                slope = spacing / jnp.maximum(spacing * spacing, 1.0)
                moved = coef - (sigma_ref[r:r + BLOCK, :] * unit - theta * coef) * slope
                moved_ref[at] = moved
                if not last:
                    refs[-1][at] = moved.astype(BF16)
                out = out + folded(moved * moved)
        put(square_ref, out)

    outs = (SDS((rows, cols), F32), ONE) + ((() if last else (SDS((rows, cols), BF16),)))
    return call(kernel, "correct", outs, (VMEM,) * len(outs), [VMEM] * (6 + len(sigmas)),
                (*corr, *weights, vector, diag, *sigmas), 12 * rows * cols, 2 ** 20)


def normalise(cells, vector, weights):
    rows, cols = vector.shape
    parts = 4
    step = rows // parts

    def kernel(weight_a, weight_b, vector_ref, out_ref, buf, sems):
        norm = lax.rsqrt(total(weight_a, weight_b) / cells + EPS)
        copies = []
        for p in range(parts):
            at = pl.ds(p * step, step)
            for r in range(p * step, (p + 1) * step, BLOCK):
                buf[r:r + BLOCK, :] = vector_ref[r:r + BLOCK, :] * norm
            copies.append(pltpu.make_async_copy(buf.at[at], out_ref.at[at], sems.at[p]))
            copies[-1].start()
        for copy in copies:
            copy.wait()

    return call(kernel, "normalise", SDS((rows, cols), F32), ANY, [VMEM] * 3, (*weights, vector),
                rows * cols, 8 * rows * cols, [pltpu.VMEM((rows, cols), F32), pltpu.SemaphoreType.DMA((parts,))])


def local(ops, cols, wave_coef, diag_energy, left, right, block_mask):
    pairs, width, _ = left.shape
    own_cols = right.shape[2]
    blocks = block_mask.shape[1]
    cells = float(width * width)
    half, quarter, size = width // 2, width // 4, own_cols // CHUNKS
    stages = ops.bit_length() - 1
    reach = float(pairs * ops * width) * TOP * TOP

    def swap(x, stage):
        pairing = []
        for o in range(ops):
            for c in range(cols):
                bit = ORDER[c % 2][stage] if stage < 2 else 1 << stage
                pairing.append((o * cols + c, (o ^ bit) * cols + c))
        return lax.ppermute(x, BOTH, pairing)

    def across(x):
        return lax.ppermute(x, "col", [(c, c ^ 1) for c in range(cols)])

    me, core = lax.axis_index("op").astype(jnp.uint32), lax.axis_index("col").astype(jnp.uint32)
    low, high = me & 1, (me >> 1) & 1
    bit0, bit1 = jnp.where(core == 0, low, high), jnp.where(core == 0, high, low)
    low_near, low_half, zero = bit1 == 0, bit0 == 0, jnp.zeros((), jnp.uint32)
    keep_at, send_at = bit1 * quarter, (1 - bit1) * quarter
    wave_coef, keep_at, send_at, low_near, low_half = lax.optimization_barrier(
        (wave_coef, keep_at, send_at, low_near, low_half))

    def begin(send):
        return swap(send.astype(F16), 0)

    def halve(keep, got):
        keep = keep + got.astype(F32)
        send = lax.dynamic_slice(keep, (send_at, zero), (quarter, size)).astype(F16)
        return send, lax.dynamic_slice(keep, (keep_at, zero), (quarter, size))

    def finish(keep, got):
        keep = keep + got.astype(F32)
        for stage in range(2, stages):
            send = keep.astype(F16)
            keep = send.astype(F32) + swap(send, stage).astype(F32)
        return keep.astype(F16)

    def gathered(piece):
        p1, p2 = swap(piece, 1), swap(piece, 0)
        p3 = lax.ppermute(piece, BOTH, [(o * cols + c, (o ^ 3) * cols + c) for o in range(ops) for c in range(cols)])
        near0, near1 = jnp.where(low_near, piece, p1), jnp.where(low_near, p1, piece)
        far0, far1 = jnp.where(low_near, p2, p3), jnp.where(low_near, p3, p2)
        return jnp.concatenate([
            jnp.where(low_half, near0, far0), jnp.where(low_half, near1, far1),
            jnp.where(low_half, far0, near0), jnp.where(low_half, far1, near1)], axis=0).astype(F32)

    vector = wave_coef
    own, weight = open_vector(wave_coef)
    mask = block_mask.reshape(-1)
    sent, right = operators(left, right, mask, blocks, True)
    for step in range(STEPS):
        other = across(own)
        weights = (weight, across(weight))
        inners, keeps, gots = [], [], []
        for c in range(CHUNKS):
            inner, send = sent_half(c, reach, weights, own, other, right, sent)
            gots.append(begin(send))
            inners.append(inner)
            own, other = lax.optimization_barrier((own, other, inner))[:2]
        inners[0], mask = lax.optimization_barrier((inners[0], mask, inners[-1]))[:2]
        if step == 0:
            kept = operators(left, right, mask, blocks, False)
        sigmas = []
        for c in range(CHUNKS):
            keep = kept_half(reach, weights, inners[c], kept)
            send, keep = halve(keep, gots[c])
            if c + 1 < CHUNKS:
                send, inners[c + 1] = lax.optimization_barrier((send, inners[c + 1]))
            sigmas.append(gathered(finish(keep, swap(send, 1))))
        corr = correlate(vector, sigmas)
        vector, weight, *own = correct(
            step == 0, step == STEPS - 1, reach, cells, vector, sigmas, diag_energy, (corr, across(corr)), weights)
        own = own[0] if own else None
    return normalise(cells, vector, (weight, across(weight)))


def solution(mesh):
    in_specs = (
        P("geom", "col"),
        P("geom", "col"),
        P(("geom", "op"), None, None),
        P(("geom", "op"), None, "col"),
        P(("geom", "op"), None, None),
    )
    body = functools.partial(local, mesh.shape["op"], mesh.shape["col"])
    return jax.shard_map(body, mesh=mesh, in_specs=in_specs, out_specs=P("geom", "col"), check_vma=False)
```

```python
import functools

import jax
import jax.numpy as jnp
from jax import lax
from jax.experimental import pallas as pl
from jax.experimental.pallas import tpu as pltpu
from jax.sharding import PartitionSpec as P

STEPS = 2
CHUNKS = 2
EPS = 1e-06
BLOCK = 16
TOP = 0.1875
BOTH = ("op", "col")
F32, F16, BF16 = jnp.float32, jnp.float16, jnp.bfloat16
SDS = jax.ShapeDtypeStruct
ANY = pl.BlockSpec(memory_space=pl.ANY)
VMEM = pl.BlockSpec(memory_space=pltpu.VMEM)
SMEM = pl.BlockSpec(memory_space=pltpu.SMEM)
ONE = SDS((8, 128), F32)
ORDER = ((1, 2), (2, 1))


def in_hbm(x):
    return pltpu.with_memory_space_constraint(x, pltpu.HBM)


def call(kernel, name, outs, out_specs, in_specs, args, flops, moved, scratch=(), mib=8):
    return pl.pallas_call(
        kernel, out_shape=outs, in_specs=in_specs, out_specs=out_specs, scratch_shapes=scratch, name=name,
        compiler_params=pltpu.CompilerParams(vmem_limit_bytes=mib * 2 ** 20),
        cost_estimate=pl.CostEstimate(flops=flops, bytes_accessed=moved, transcendentals=0))(*args)


def total(own_ref, other_ref):
    return own_ref[:1, :1] + other_ref[:1, :1]


def put(ref, parts):
    ref[...] = jnp.full(ref.shape, jnp.sum(parts), F32)


def folded(block):
    return jnp.sum(block.reshape(block.shape[0] // 8, 8, block.shape[1]), axis=0)


def scale_of(reach, weight):
    return 32768.0 / (reach * (jnp.sqrt(weight) + 1e-30))


def open_vector(coef):
    rows, cols = coef.shape
    parts = 8
    step = rows // parts

    def kernel(coef_ref, wave_ref, weight_ref, buf, sems):
        copies = []
        for p in range(parts):
            at = pl.ds(p * step, step)
            copies.append(pltpu.make_async_copy(coef_ref.at[at], buf.at[at], sems.at[p]))
            copies[-1].start()
        weight = jnp.zeros((8, cols), F32)
        for p in range(parts):
            copies[p].wait()
            for r in range(p * step, (p + 1) * step, BLOCK):
                block = buf[r:r + BLOCK, :]
                wave_ref[r:r + BLOCK, :] = block.astype(BF16)
                weight = weight + folded(block * block)
        put(weight_ref, weight)

    return call(kernel, "open_vector", (SDS((rows, cols), BF16), ONE), (VMEM, VMEM), [ANY], (in_hbm(coef),),
                3 * rows * cols, 8 * rows * cols,
                [pltpu.VMEM((rows, cols), F32), pltpu.SemaphoreType.DMA((parts,))], mib=12)


def first_half():
    me, core = lax.axis_index("op"), lax.axis_index("col")
    bit = 0
    for c, (mask, _) in enumerate(ORDER):
        bit = bit + jnp.where(core == c, (me // mask) % 2, 0)
    return 1 - bit


def operators(left, mask, blocks, sent):
    pairs, width, _ = left.shape
    half, inside = width // 2, width // blocks
    strips = half // inside

    def kernel(mask_ref, left_ref, out_ref, buf, sems):
        h = first_half() if sent else 1 - first_half()
        order = [(k, i) for k in range(pairs) for i in range(strips)]
        copies = []
        for n, (k, i) in enumerate(order):
            copies.append(pltpu.make_async_copy(
                left_ref.at[k, pl.ds(pl.multiple_of(h * half + i * inside, inside), inside)], buf.at[n], sems.at[n]))
            copies[-1].start()
        for n, (k, i) in enumerate(order):
            copies[n].wait()
            for j in range(blocks):
                keep = mask_ref[(k * blocks + h * strips + i) * blocks + j]
                block = buf[n, :, j * inside:(j + 1) * inside]
                out_ref[i * inside:(i + 1) * inside, k * width + j * inside:k * width + (j + 1) * inside] = (
                    jnp.where(keep != 0, block, jnp.zeros_like(block)))

    count = pairs * strips
    return call(kernel, "sent_operators" if sent else "kept_operators", SDS((half, pairs * width), BF16), VMEM,
                [SMEM, ANY], (mask, in_hbm(left)), left.size, 2 * left.size,
                [pltpu.VMEM((count, inside, width), BF16), pltpu.SemaphoreType.DMA((count,))], mib=12)


def product(out_ref, scale, left_ref, right_ref, parts):
    step = left_ref.shape[0] // parts
    for p in range(parts):
        rows = slice(p * step, (p + 1) * step)
        out_ref[rows, :] = scale * jnp.dot(left_ref[rows, :], right_ref[...], preferred_element_type=F32)


def sent_half(chunk, reach, weights, own, other, right, masked):
    pairs, width, cols = right.shape
    size, half = cols // CHUNKS, width // 2
    at = slice(chunk * size, (chunk + 1) * size)
    step = width // 4

    def kernel(a_ref, b_ref, own_ref, other_ref, right_ref, masked_ref, inner_ref, send_ref):
        core = lax.axis_index("col")
        here = pl.ds(pl.multiple_of(core * cols, cols), cols)
        there = pl.ds(pl.multiple_of((1 - core) * cols, cols), cols)
        scale = scale_of(reach, total(a_ref, b_ref))
        for k in range(pairs):
            near, far = right_ref[k, here, at], right_ref[k, there, at]
            for r in range(0, width, step):
                inner_ref[k * width + r:k * width + r + step, :] = (
                    jnp.dot(own_ref[r:r + step, :], near, preferred_element_type=F32)
                    + jnp.dot(other_ref[r:r + step, :], far, preferred_element_type=F32)).astype(BF16)
        product(send_ref, scale, masked_ref, inner_ref, 2)

    return call(kernel, "sent_half_%d" % chunk, (SDS((pairs * width, size), BF16), SDS((half, size), F32)),
                (VMEM, VMEM), [VMEM] * 6, (*weights, own, other, right, masked),
                3 * pairs * width * width * size, 2 ** 20)


def kept_half(reach, weights, inner, masked):
    half, depth = masked.shape
    size = inner.shape[1]

    def kernel(a_ref, b_ref, inner_ref, masked_ref, keep_ref):
        product(keep_ref, scale_of(reach, total(a_ref, b_ref)), masked_ref, inner_ref, 2)

    return call(kernel, "kept_half", SDS((half, size), F32), VMEM, [VMEM] * 4,
                (*weights, inner, masked), 2 * half * depth * size, 2 ** 20)


def correlate(vector, sigmas):
    rows, cols = vector.shape
    size = cols // len(sigmas)

    def kernel(vector_ref, *refs):
        out = jnp.zeros((8, size), F32)
        for r in range(0, rows, BLOCK):
            for c, sigma_ref in enumerate(refs[:-1]):
                out = out + folded(vector_ref[r:r + BLOCK, c * size:(c + 1) * size] * sigma_ref[r:r + BLOCK, :])
        put(refs[-1], out)

    return call(kernel, "correlate", ONE, VMEM, [VMEM] * (1 + len(sigmas)), (vector, *sigmas), 2 * rows * cols, 2 ** 20)


def correct(first, last, reach, cells, vector, sigmas, diag, corr, weights):
    rows, cols = vector.shape
    size = cols // len(sigmas)

    def kernel(corr_a, corr_b, weight_a, weight_b, vector_ref, diag_ref, *refs):
        sigma_refs, (moved_ref, square_ref) = refs[:len(sigmas)], refs[len(sigmas):len(sigmas) + 2]
        weight = total(weight_a, weight_b)
        scale = scale_of(reach, weight)
        norm = jnp.ones((1, 1), F32) if first else lax.rsqrt(weight / cells + EPS)
        square = norm * norm
        theta = (total(corr_a, corr_b) / scale * square / cells) / (weight * square / cells + EPS)
        unit = norm / scale
        out = jnp.zeros((8, size), F32)
        for r in range(0, rows, BLOCK):
            for c, sigma_ref in enumerate(sigma_refs):
                at = (slice(r, r + BLOCK), slice(c * size, (c + 1) * size))
                coef = vector_ref[at] * norm
                spacing = diag_ref[at] - theta
                slope = spacing / jnp.maximum(spacing * spacing, 1.0)
                moved = coef - (sigma_ref[r:r + BLOCK, :] * unit - theta * coef) * slope
                moved_ref[at] = moved
                if not last:
                    refs[-1][at] = moved.astype(BF16)
                out = out + folded(moved * moved)
        put(square_ref, out)

    outs = (SDS((rows, cols), F32), ONE) + ((() if last else (SDS((rows, cols), BF16),)))
    return call(kernel, "correct", outs, (VMEM,) * len(outs), [VMEM] * (6 + len(sigmas)),
                (*corr, *weights, vector, diag, *sigmas), 12 * rows * cols, 2 ** 20)


def normalise(cells, vector, weights):
    rows, cols = vector.shape
    parts = 8
    step = rows // parts

    def kernel(weight_a, weight_b, vector_ref, out_ref, buf, sems):
        norm = lax.rsqrt(total(weight_a, weight_b) / cells + EPS)
        copies = []
        for p in range(parts):
            at = pl.ds(p * step, step)
            for r in range(p * step, (p + 1) * step, BLOCK):
                buf[r:r + BLOCK, :] = vector_ref[r:r + BLOCK, :] * norm
            copies.append(pltpu.make_async_copy(buf.at[at], out_ref.at[at], sems.at[p]))
            copies[-1].start()
        for copy in copies:
            copy.wait()

    return call(kernel, "normalise", SDS((rows, cols), F32), ANY, [VMEM] * 3, (*weights, vector),
                rows * cols, 8 * rows * cols, [pltpu.VMEM((rows, cols), F32), pltpu.SemaphoreType.DMA((parts,))])


def local(ops, cols, wave_coef, diag_energy, left, right, block_mask):
    pairs, width, _ = left.shape
    own_cols = right.shape[2]
    blocks = block_mask.shape[1]
    cells = float(width * width)
    half, quarter, size = width // 2, width // 4, own_cols // CHUNKS
    stages = ops.bit_length() - 1
    reach = float(pairs * ops * width) * TOP * TOP

    def swap(x, stage):
        pairing = []
        for o in range(ops):
            for c in range(cols):
                bit = ORDER[c % 2][stage] if stage < 2 else 1 << stage
                pairing.append((o * cols + c, (o ^ bit) * cols + c))
        return lax.ppermute(x, BOTH, pairing)

    def across(x):
        return lax.ppermute(x, "col", [(c, c ^ 1) for c in range(cols)])

    me, core = lax.axis_index("op").astype(jnp.uint32), lax.axis_index("col").astype(jnp.uint32)
    low, high = me & 1, (me >> 1) & 1
    bit0, bit1 = jnp.where(core == 0, low, high), jnp.where(core == 0, high, low)
    low_near, low_half, zero = bit1 == 0, bit0 == 0, jnp.zeros((), jnp.uint32)
    keep_at, send_at = bit1 * quarter, (1 - bit1) * quarter
    wave_coef, keep_at, send_at, low_near, low_half = lax.optimization_barrier(
        (wave_coef, keep_at, send_at, low_near, low_half))

    def begin(send):
        return swap(send.astype(F16), 0)

    def halve(keep, got):
        keep = keep + got.astype(F32)
        send = lax.dynamic_slice(keep, (send_at, zero), (quarter, size)).astype(F16)
        return send, lax.dynamic_slice(keep, (keep_at, zero), (quarter, size))

    def finish(keep, got):
        keep = keep + got.astype(F32)
        for stage in range(2, stages):
            send = keep.astype(F16)
            keep = send.astype(F32) + swap(send, stage).astype(F32)
        return keep.astype(F16)

    def gathered(piece):
        p3 = lax.ppermute(piece, BOTH, [(o * cols + c, (o ^ 3) * cols + c) for o in range(ops) for c in range(cols)])
        p1, p2 = swap(piece, 1), swap(piece, 0)
        near0, near1 = jnp.where(low_near, piece, p1), jnp.where(low_near, p1, piece)
        far0, far1 = jnp.where(low_near, p2, p3), jnp.where(low_near, p3, p2)
        return jnp.concatenate([
            jnp.where(low_half, near0, far0), jnp.where(low_half, near1, far1),
            jnp.where(low_half, far0, near0), jnp.where(low_half, far1, near1)], axis=0).astype(F32)

    vector = wave_coef
    own, weight = open_vector(wave_coef)
    mask = block_mask.reshape(-1)
    sent = operators(left, mask, blocks, True)
    for step in range(STEPS):
        other = across(own)
        weights = (weight, across(weight))
        inners, keeps, gots = [], [], []
        for c in range(CHUNKS):
            inner, send = sent_half(c, reach, weights, own, other, right, sent)
            gots.append(begin(send))
            inners.append(inner)
            own, other = lax.optimization_barrier((own, other, inner))[:2]
        inners[0], mask = lax.optimization_barrier((inners[0], mask, inners[-1]))[:2]
        if step == 0:
            kept = operators(left, mask, blocks, False)
        sigmas = []
        for c in range(CHUNKS):
            keep = kept_half(reach, weights, inners[c], kept)
            send, keep = halve(keep, gots[c])
            if c + 1 < CHUNKS:
                send, inners[c + 1] = lax.optimization_barrier((send, inners[c + 1]))
            sigmas.append(gathered(finish(keep, swap(send, 1))))
        corr = correlate(vector, sigmas)
        vector, weight, *own = correct(
            step == 0, step == STEPS - 1, reach, cells, vector, sigmas, diag_energy, (corr, across(corr)), weights)
        own = own[0] if own else None
    return normalise(cells, vector, (weight, across(weight)))


def solution(mesh):
    in_specs = (
        P("geom", "col"),
        P("geom", "col"),
        P(("geom", "op"), None, None),
        P(("geom", "op"), None, "col"),
        P(("geom", "op"), None, None),
    )
    body = functools.partial(local, mesh.shape["op"], mesh.shape["col"])
    return jax.shard_map(body, mesh=mesh, in_specs=in_specs, out_specs=P("geom", "col"), check_vma=False)
```

```python
import functools

import jax
import jax.numpy as jnp
from jax import lax
from jax.experimental import pallas as pl
from jax.experimental.pallas import tpu as pltpu
from jax.sharding import PartitionSpec as P

STEPS = 2
CHUNKS = 2
EPS = 1e-06
BLOCK = 16
TOP = 0.1875
BOTH = ("op", "col")
F32, F16, BF16 = jnp.float32, jnp.float16, jnp.bfloat16
SDS = jax.ShapeDtypeStruct
ANY = pl.BlockSpec(memory_space=pl.ANY)
VMEM = pl.BlockSpec(memory_space=pltpu.VMEM)
SMEM = pl.BlockSpec(memory_space=pltpu.SMEM)
ONE = SDS((8, 128), F32)
ORDER = ((1, 2), (2, 1))


def in_hbm(x):
    return pltpu.with_memory_space_constraint(x, pltpu.HBM)


def call(kernel, name, outs, out_specs, in_specs, args, flops, moved, scratch=(), mib=8):
    return pl.pallas_call(
        kernel, out_shape=outs, in_specs=in_specs, out_specs=out_specs, scratch_shapes=scratch, name=name,
        compiler_params=pltpu.CompilerParams(vmem_limit_bytes=mib * 2 ** 20),
        cost_estimate=pl.CostEstimate(flops=flops, bytes_accessed=moved, transcendentals=0))(*args)


def total(own_ref, other_ref):
    return own_ref[:1, :1] + other_ref[:1, :1]


def put(ref, parts):
    ref[...] = jnp.full(ref.shape, jnp.sum(parts), F32)


def folded(block):
    return jnp.sum(block.reshape(block.shape[0] // 8, 8, block.shape[1]), axis=0)


def scale_of(reach, weight):
    return 32768.0 / (reach * (jnp.sqrt(weight) + 1e-30))


def open_vector(coef):
    rows, cols = coef.shape
    parts = 8
    step = rows // parts

    def kernel(coef_ref, wave_ref, weight_ref, buf, sems):
        copies = []
        for p in range(parts):
            at = pl.ds(p * step, step)
            copies.append(pltpu.make_async_copy(coef_ref.at[at], buf.at[at], sems.at[p]))
            copies[-1].start()
        weight = jnp.zeros((8, cols), F32)
        for p in range(parts):
            copies[p].wait()
            for r in range(p * step, (p + 1) * step, BLOCK):
                block = buf[r:r + BLOCK, :]
                wave_ref[r:r + BLOCK, :] = block.astype(BF16)
                weight = weight + folded(block * block)
        put(weight_ref, weight)

    return call(kernel, "open_vector", (SDS((rows, cols), BF16), ONE), (VMEM, VMEM), [ANY], (in_hbm(coef),),
                3 * rows * cols, 8 * rows * cols,
                [pltpu.VMEM((rows, cols), F32), pltpu.SemaphoreType.DMA((parts,))], mib=12)


def first_half():
    me, core = lax.axis_index("op"), lax.axis_index("col")
    bit = 0
    for c, (mask, _) in enumerate(ORDER):
        place = me // mask + (me // 4 if mask == 2 else 0)
        bit = bit + jnp.where(core == c, place % 2, 0)
    return 1 - bit


def operators(left, mask, blocks, sent):
    pairs, width, _ = left.shape
    half, inside = width // 2, width // blocks
    strips = half // inside

    def kernel(mask_ref, left_ref, out_ref, buf, sems):
        h = first_half() if sent else 1 - first_half()
        order = [(k, i) for k in range(pairs) for i in range(strips)]
        copies = []
        for n, (k, i) in enumerate(order):
            copies.append(pltpu.make_async_copy(
                left_ref.at[k, pl.ds(pl.multiple_of(h * half + i * inside, inside), inside)], buf.at[n], sems.at[n]))
            copies[-1].start()
        for n, (k, i) in enumerate(order):
            copies[n].wait()
            for j in range(blocks):
                keep = mask_ref[(k * blocks + h * strips + i) * blocks + j]
                block = buf[n, :, j * inside:(j + 1) * inside]
                out_ref[i * inside:(i + 1) * inside, k * width + j * inside:k * width + (j + 1) * inside] = (
                    jnp.where(keep != 0, block, jnp.zeros_like(block)))

    count = pairs * strips
    return call(kernel, "sent_operators" if sent else "kept_operators", SDS((half, pairs * width), BF16), VMEM,
                [SMEM, ANY], (mask, in_hbm(left)), left.size, 2 * left.size,
                [pltpu.VMEM((count, inside, width), BF16), pltpu.SemaphoreType.DMA((count,))], mib=12)


def product(out_ref, scale, left_ref, right_ref, parts):
    step = left_ref.shape[0] // parts
    for p in range(parts):
        rows = slice(p * step, (p + 1) * step)
        out_ref[rows, :] = scale * jnp.dot(left_ref[rows, :], right_ref[...], preferred_element_type=F32)


def sent_half(chunk, reach, weights, own, other, right, masked):
    pairs, width, cols = right.shape
    size, half = cols // CHUNKS, width // 2
    at = slice(chunk * size, (chunk + 1) * size)
    step = width // 4

    def kernel(a_ref, b_ref, own_ref, other_ref, right_ref, masked_ref, inner_ref, send_ref):
        core = lax.axis_index("col")
        here = pl.ds(pl.multiple_of(core * cols, cols), cols)
        there = pl.ds(pl.multiple_of((1 - core) * cols, cols), cols)
        scale = scale_of(reach, total(a_ref, b_ref))
        for k in range(pairs):
            near, far = right_ref[k, here, at], right_ref[k, there, at]
            for r in range(0, width, step):
                inner_ref[k * width + r:k * width + r + step, :] = (
                    jnp.dot(own_ref[r:r + step, :], near, preferred_element_type=F32)
                    + jnp.dot(other_ref[r:r + step, :], far, preferred_element_type=F32)).astype(BF16)
        product(send_ref, scale, masked_ref, inner_ref, 2)

    return call(kernel, "sent_half_%d" % chunk, (SDS((pairs * width, size), BF16), SDS((half, size), F32)),
                (VMEM, VMEM), [VMEM] * 6, (*weights, own, other, right, masked),
                3 * pairs * width * width * size, 2 ** 20)


def kept_half(reach, weights, inner, masked):
    half, depth = masked.shape
    size = inner.shape[1]

    def kernel(a_ref, b_ref, inner_ref, masked_ref, keep_ref):
        product(keep_ref, scale_of(reach, total(a_ref, b_ref)), masked_ref, inner_ref, 2)

    return call(kernel, "kept_half", SDS((half, size), F32), VMEM, [VMEM] * 4,
                (*weights, inner, masked), 2 * half * depth * size, 2 ** 20)


def correlate(vector, sigmas):
    rows, cols = vector.shape
    size = cols // len(sigmas)

    def kernel(vector_ref, *refs):
        out = jnp.zeros((8, size), F32)
        for r in range(0, rows, BLOCK):
            for c, sigma_ref in enumerate(refs[:-1]):
                out = out + folded(vector_ref[r:r + BLOCK, c * size:(c + 1) * size] * sigma_ref[r:r + BLOCK, :])
        put(refs[-1], out)

    return call(kernel, "correlate", ONE, VMEM, [VMEM] * (1 + len(sigmas)), (vector, *sigmas), 2 * rows * cols, 2 ** 20)


def correct(first, last, reach, cells, vector, sigmas, diag, corr, weights):
    rows, cols = vector.shape
    size = cols // len(sigmas)

    def kernel(corr_a, corr_b, weight_a, weight_b, vector_ref, diag_ref, *refs):
        sigma_refs, (moved_ref, square_ref) = refs[:len(sigmas)], refs[len(sigmas):len(sigmas) + 2]
        weight = total(weight_a, weight_b)
        scale = scale_of(reach, weight)
        norm = jnp.ones((1, 1), F32) if first else lax.rsqrt(weight / cells + EPS)
        square = norm * norm
        theta = (total(corr_a, corr_b) / scale * square / cells) / (weight * square / cells + EPS)
        unit = norm / scale
        out = jnp.zeros((8, size), F32)
        for r in range(0, rows, BLOCK):
            for c, sigma_ref in enumerate(sigma_refs):
                at = (slice(r, r + BLOCK), slice(c * size, (c + 1) * size))
                coef = vector_ref[at] * norm
                spacing = diag_ref[at] - theta
                slope = spacing / jnp.maximum(spacing * spacing, 1.0)
                moved = coef - (sigma_ref[r:r + BLOCK, :] * unit - theta * coef) * slope
                moved_ref[at] = moved
                if not last:
                    refs[-1][at] = moved.astype(BF16)
                out = out + folded(moved * moved)
        put(square_ref, out)

    outs = (SDS((rows, cols), F32), ONE) + ((() if last else (SDS((rows, cols), BF16),)))
    return call(kernel, "correct", outs, (VMEM,) * len(outs), [VMEM] * (6 + len(sigmas)),
                (*corr, *weights, vector, diag, *sigmas), 12 * rows * cols, 2 ** 20)


def normalise(cells, vector, weights):
    rows, cols = vector.shape
    parts = 8
    step = rows // parts

    def kernel(weight_a, weight_b, vector_ref, out_ref, buf, sems):
        norm = lax.rsqrt(total(weight_a, weight_b) / cells + EPS)
        copies = []
        for p in range(parts):
            at = pl.ds(p * step, step)
            for r in range(p * step, (p + 1) * step, BLOCK):
                buf[r:r + BLOCK, :] = vector_ref[r:r + BLOCK, :] * norm
            copies.append(pltpu.make_async_copy(buf.at[at], out_ref.at[at], sems.at[p]))
            copies[-1].start()
        for copy in copies:
            copy.wait()

    return call(kernel, "normalise", SDS((rows, cols), F32), ANY, [VMEM] * 3, (*weights, vector),
                rows * cols, 8 * rows * cols, [pltpu.VMEM((rows, cols), F32), pltpu.SemaphoreType.DMA((parts,))])


def local(ops, cols, wave_coef, diag_energy, left, right, block_mask):
    pairs, width, _ = left.shape
    own_cols = right.shape[2]
    blocks = block_mask.shape[1]
    cells = float(width * width)
    half, quarter, size = width // 2, width // 4, own_cols // CHUNKS
    stages = ops.bit_length() - 1
    reach = float(pairs * ops * width) * TOP * TOP

    def swap(x, stage):
        pairing = []
        for o in range(ops):
            for c in range(cols):
                bit = (*ORDER[c % 2], 6)[stage] if stage < 3 else 1 << stage
                pairing.append((o * cols + c, (o ^ bit) * cols + c))
        return lax.ppermute(x, BOTH, pairing)

    def across(x):
        return lax.ppermute(x, "col", [(c, c ^ 1) for c in range(cols)])

    me, core = lax.axis_index("op").astype(jnp.uint32), lax.axis_index("col").astype(jnp.uint32)
    low, high = me & 1, ((me >> 1) ^ (me >> 2)) & 1
    bit0, bit1 = jnp.where(core == 0, low, high), jnp.where(core == 0, high, low)
    low_near, low_half, zero = bit1 == 0, bit0 == 0, jnp.zeros((), jnp.uint32)
    keep_at, send_at = bit1 * quarter, (1 - bit1) * quarter
    wave_coef, keep_at, send_at, low_near, low_half = lax.optimization_barrier(
        (wave_coef, keep_at, send_at, low_near, low_half))

    def begin(send):
        return swap(send.astype(F16), 0)

    def halve(keep, got):
        keep = keep + got.astype(F32)
        send = lax.dynamic_slice(keep, (send_at, zero), (quarter, size)).astype(F16)
        return send, lax.dynamic_slice(keep, (keep_at, zero), (quarter, size))

    def finish(keep, got):
        keep = keep + got.astype(F32)
        for stage in range(2, stages):
            send = keep.astype(F16)
            keep = send.astype(F32) + swap(send, stage).astype(F32)
        return keep.astype(F16)

    def gathered(piece):
        p3 = lax.ppermute(piece, BOTH, [(o * cols + c, (o ^ 3) * cols + c) for o in range(ops) for c in range(cols)])
        p1, p2 = swap(piece, 1), swap(piece, 0)
        near0, near1 = jnp.where(low_near, piece, p1), jnp.where(low_near, p1, piece)
        far0, far1 = jnp.where(low_near, p2, p3), jnp.where(low_near, p3, p2)
        return jnp.concatenate([
            jnp.where(low_half, near0, far0), jnp.where(low_half, near1, far1),
            jnp.where(low_half, far0, near0), jnp.where(low_half, far1, near1)], axis=0).astype(F32)

    vector = wave_coef
    own, weight = open_vector(wave_coef)
    mask = block_mask.reshape(-1)
    sent = operators(left, mask, blocks, True)
    for step in range(STEPS):
        other = across(own)
        weights = (weight, across(weight))
        inners, keeps, gots = [], [], []
        for c in range(CHUNKS):
            inner, send = sent_half(c, reach, weights, own, other, right, sent)
            gots.append(begin(send))
            inners.append(inner)
            own, other = lax.optimization_barrier((own, other, inner))[:2]
        inners[0], mask = lax.optimization_barrier((inners[0], mask, inners[-1]))[:2]
        if step == 0:
            kept = operators(left, mask, blocks, False)
        sigmas = []
        for c in range(CHUNKS):
            keep = kept_half(reach, weights, inners[c], kept)
            send, keep = halve(keep, gots[c])
            if c + 1 < CHUNKS:
                send, inners[c + 1] = lax.optimization_barrier((send, inners[c + 1]))
            sigmas.append(gathered(finish(keep, swap(send, 1))))
        corr = correlate(vector, sigmas)
        vector, weight, *own = correct(
            step == 0, step == STEPS - 1, reach, cells, vector, sigmas, diag_energy, (corr, across(corr)), weights)
        own = own[0] if own else None
    return normalise(cells, vector, (weight, across(weight)))


def solution(mesh):
    in_specs = (
        P("geom", "col"),
        P("geom", "col"),
        P(("geom", "op"), None, None),
        P(("geom", "op"), None, "col"),
        P(("geom", "op"), None, None),
    )
    body = functools.partial(local, mesh.shape["op"], mesh.shape["col"])
    return jax.shard_map(body, mesh=mesh, in_specs=in_specs, out_specs=P("geom", "col"), check_vma=False)
```

```python
import functools

import jax
import jax.numpy as jnp
from jax import lax
from jax.experimental import pallas as pl
from jax.experimental.pallas import tpu as pltpu
from jax.sharding import PartitionSpec as P

STEPS = 2
CHUNKS = 2
EPS = 1e-06
BLOCK = 16
TOP = 0.1875
BOTH = ("op", "col")
F32, F16, BF16 = jnp.float32, jnp.float16, jnp.bfloat16
SDS = jax.ShapeDtypeStruct
ANY = pl.BlockSpec(memory_space=pl.ANY)
VMEM = pl.BlockSpec(memory_space=pltpu.VMEM)
SMEM = pl.BlockSpec(memory_space=pltpu.SMEM)
ONE = SDS((8, 128), F32)
ORDER = ((1, 2), (2, 1))


def in_hbm(x):
    return pltpu.with_memory_space_constraint(x, pltpu.HBM)


def call(kernel, name, outs, out_specs, in_specs, args, flops, moved, scratch=(), mib=8):
    return pl.pallas_call(
        kernel, out_shape=outs, in_specs=in_specs, out_specs=out_specs, scratch_shapes=scratch, name=name,
        compiler_params=pltpu.CompilerParams(vmem_limit_bytes=mib * 2 ** 20),
        cost_estimate=pl.CostEstimate(flops=flops, bytes_accessed=moved, transcendentals=0))(*args)


def total(own_ref, other_ref):
    return own_ref[:1, :1] + other_ref[:1, :1]


def put(ref, parts):
    ref[...] = jnp.full(ref.shape, jnp.sum(parts), F32)


def folded(block):
    return jnp.sum(block.reshape(block.shape[0] // 8, 8, block.shape[1]), axis=0)


def scale_of(reach, weight):
    return 32768.0 / (reach * (jnp.sqrt(weight) + 1e-30))


def open_vector(coef):
    rows, cols = coef.shape
    parts = 8
    step = rows // parts

    def kernel(coef_ref, wave_ref, weight_ref, buf, sems):
        copies = []
        for p in range(parts):
            at = pl.ds(p * step, step)
            copies.append(pltpu.make_async_copy(coef_ref.at[at], buf.at[at], sems.at[p]))
            copies[-1].start()
        weight = jnp.zeros((8, cols), F32)
        for p in range(parts):
            copies[p].wait()
            for r in range(p * step, (p + 1) * step, BLOCK):
                block = buf[r:r + BLOCK, :]
                wave_ref[r:r + BLOCK, :] = block.astype(BF16)
                weight = weight + folded(block * block)
        put(weight_ref, weight)

    return call(kernel, "open_vector", (SDS((rows, cols), BF16), ONE), (VMEM, VMEM), [ANY], (in_hbm(coef),),
                3 * rows * cols, 8 * rows * cols,
                [pltpu.VMEM((rows, cols), F32), pltpu.SemaphoreType.DMA((parts,))], mib=12)


def first_half():
    me, core = lax.axis_index("op"), lax.axis_index("col")
    bit = 0
    for c, (mask, _) in enumerate(ORDER):
        place = me // mask + (me // 4 if mask == 2 else 0)
        bit = bit + jnp.where(core == c, place % 2, 0)
    return 1 - bit


def operators(left, mask, blocks, sent):
    pairs, width, _ = left.shape
    half, inside = width // 2, width // blocks
    strips = half // inside

    def kernel(mask_ref, left_ref, out_ref, buf, sems):
        h = first_half() if sent else 1 - first_half()
        order = [(k, i) for k in range(pairs) for i in range(strips)]
        copies = []
        for n, (k, i) in enumerate(order):
            copies.append(pltpu.make_async_copy(
                left_ref.at[k, pl.ds(pl.multiple_of(h * half + i * inside, inside), inside)], buf.at[n], sems.at[n]))
            copies[-1].start()
        for n, (k, i) in enumerate(order):
            copies[n].wait()
            for j in range(blocks):
                keep = mask_ref[(k * blocks + h * strips + i) * blocks + j]
                block = buf[n, :, j * inside:(j + 1) * inside]
                out_ref[i * inside:(i + 1) * inside, k * width + j * inside:k * width + (j + 1) * inside] = (
                    jnp.where(keep != 0, block, jnp.zeros_like(block)))

    count = pairs * strips
    return call(kernel, "sent_operators" if sent else "kept_operators", SDS((half, pairs * width), BF16), VMEM,
                [SMEM, ANY], (mask, in_hbm(left)), left.size, 2 * left.size,
                [pltpu.VMEM((count, inside, width), BF16), pltpu.SemaphoreType.DMA((count,))], mib=12)


def product(out_ref, scale, left_ref, right_ref, parts):
    step = left_ref.shape[0] // parts
    for p in range(parts):
        rows = slice(p * step, (p + 1) * step)
        out_ref[rows, :] = scale * jnp.dot(left_ref[rows, :], right_ref[...], preferred_element_type=F32)


def own_part(own, right):
    pairs, width, cols = right.shape
    step = width // 4

    def kernel(own_ref, right_ref, part_ref):
        here = pl.ds(pl.multiple_of(lax.axis_index("col") * cols, cols), cols)
        for k in range(pairs):
            near = right_ref[k, here, :]
            for r in range(0, width, step):
                part_ref[k * width + r:k * width + r + step, :] = jnp.dot(
                    own_ref[r:r + step, :], near, preferred_element_type=F32)

    return call(kernel, "own_part", SDS((pairs * width, cols), F32), VMEM, [VMEM] * 2, (own, right),
                2 * pairs * width * cols * cols, 2 ** 20)


def sent_half(chunk, reach, weights, own, other, right, masked, part):
    pairs, width, cols = right.shape
    size, half = cols // CHUNKS, width // 2
    at = slice(chunk * size, (chunk + 1) * size)
    step = width // 4

    def kernel(a_ref, b_ref, own_ref, other_ref, right_ref, masked_ref, inner_ref, send_ref):
        core = lax.axis_index("col")
        here = pl.ds(pl.multiple_of(core * cols, cols), cols)
        there = pl.ds(pl.multiple_of((1 - core) * cols, cols), cols)
        scale = scale_of(reach, total(a_ref, b_ref))
        for k in range(pairs):
            near, far = right_ref[k, here, at], right_ref[k, there, at]
            for r in range(0, width, step):
                rows = slice(k * width + r, k * width + r + step)
                inner_ref[rows, :] = (
                    (jnp.dot(own_ref[r:r + step, :], near, preferred_element_type=F32) if part is None
                     else own_ref[rows, at])
                    + jnp.dot(other_ref[r:r + step, :], far, preferred_element_type=F32)).astype(BF16)
        product(send_ref, scale, masked_ref, inner_ref, 2)

    return call(kernel, "sent_half_%d" % chunk, (SDS((pairs * width, size), BF16), SDS((half, size), F32)),
                (VMEM, VMEM), [VMEM] * 6,
                (*weights, own if part is None else part, other, right, masked),
                3 * pairs * width * width * size, 2 ** 20)


def kept_half(reach, weights, inner, masked):
    half, depth = masked.shape
    size = inner.shape[1]

    def kernel(a_ref, b_ref, inner_ref, masked_ref, keep_ref):
        product(keep_ref, scale_of(reach, total(a_ref, b_ref)), masked_ref, inner_ref, 2)

    return call(kernel, "kept_half", SDS((half, size), F32), VMEM, [VMEM] * 4,
                (*weights, inner, masked), 2 * half * depth * size, 2 ** 20)


def correlate(vector, sigmas):
    rows, cols = vector.shape
    size = cols // len(sigmas)

    def kernel(vector_ref, *refs):
        out = jnp.zeros((8, size), F32)
        for r in range(0, rows, BLOCK):
            for c, sigma_ref in enumerate(refs[:-1]):
                out = out + folded(vector_ref[r:r + BLOCK, c * size:(c + 1) * size] * sigma_ref[r:r + BLOCK, :])
        put(refs[-1], out)

    return call(kernel, "correlate", ONE, VMEM, [VMEM] * (1 + len(sigmas)), (vector, *sigmas), 2 * rows * cols, 2 ** 20)


def correct(first, last, reach, cells, vector, sigmas, diag, corr, weights):
    rows, cols = vector.shape
    size = cols // len(sigmas)

    def kernel(corr_a, corr_b, weight_a, weight_b, vector_ref, diag_ref, *refs):
        sigma_refs, (moved_ref, square_ref) = refs[:len(sigmas)], refs[len(sigmas):len(sigmas) + 2]
        weight = total(weight_a, weight_b)
        scale = scale_of(reach, weight)
        norm = jnp.ones((1, 1), F32) if first else lax.rsqrt(weight / cells + EPS)
        square = norm * norm
        theta = (total(corr_a, corr_b) / scale * square / cells) / (weight * square / cells + EPS)
        unit = norm / scale
        out = jnp.zeros((8, size), F32)
        for r in range(0, rows, BLOCK):
            for c, sigma_ref in enumerate(sigma_refs):
                at = (slice(r, r + BLOCK), slice(c * size, (c + 1) * size))
                coef = vector_ref[at] * norm
                spacing = diag_ref[at] - theta
                slope = spacing / jnp.maximum(spacing * spacing, 1.0)
                moved = coef - (sigma_ref[r:r + BLOCK, :] * unit - theta * coef) * slope
                moved_ref[at] = moved
                if not last:
                    refs[-1][at] = moved.astype(BF16)
                out = out + folded(moved * moved)
        put(square_ref, out)

    outs = (SDS((rows, cols), F32), ONE) + ((() if last else (SDS((rows, cols), BF16),)))
    return call(kernel, "correct", outs, (VMEM,) * len(outs), [VMEM] * (6 + len(sigmas)),
                (*corr, *weights, vector, diag, *sigmas), 12 * rows * cols, 2 ** 20)


def normalise(cells, vector, weights):
    rows, cols = vector.shape
    parts = 8
    step = rows // parts

    def kernel(weight_a, weight_b, vector_ref, out_ref, buf, sems):
        norm = lax.rsqrt(total(weight_a, weight_b) / cells + EPS)
        copies = []
        for p in range(parts):
            at = pl.ds(p * step, step)
            for r in range(p * step, (p + 1) * step, BLOCK):
                buf[r:r + BLOCK, :] = vector_ref[r:r + BLOCK, :] * norm
            copies.append(pltpu.make_async_copy(buf.at[at], out_ref.at[at], sems.at[p]))
            copies[-1].start()
        for copy in copies:
            copy.wait()

    return call(kernel, "normalise", SDS((rows, cols), F32), ANY, [VMEM] * 3, (*weights, vector),
                rows * cols, 8 * rows * cols, [pltpu.VMEM((rows, cols), F32), pltpu.SemaphoreType.DMA((parts,))])


def local(ops, cols, wave_coef, diag_energy, left, right, block_mask):
    pairs, width, _ = left.shape
    own_cols = right.shape[2]
    blocks = block_mask.shape[1]
    cells = float(width * width)
    half, quarter, size = width // 2, width // 4, own_cols // CHUNKS
    stages = ops.bit_length() - 1
    reach = float(pairs * ops * width) * TOP * TOP

    def swap(x, stage):
        pairing = []
        for o in range(ops):
            for c in range(cols):
                bit = (*ORDER[c % 2], 6)[stage] if stage < 3 else 1 << stage
                pairing.append((o * cols + c, (o ^ bit) * cols + c))
        return lax.ppermute(x, BOTH, pairing)

    def across(x):
        return lax.ppermute(x, "col", [(c, c ^ 1) for c in range(cols)])

    me, core = lax.axis_index("op").astype(jnp.uint32), lax.axis_index("col").astype(jnp.uint32)
    low, high = me & 1, ((me >> 1) ^ (me >> 2)) & 1
    bit0, bit1 = jnp.where(core == 0, low, high), jnp.where(core == 0, high, low)
    low_near, low_half, zero = bit1 == 0, bit0 == 0, jnp.zeros((), jnp.uint32)
    keep_at, send_at = bit1 * quarter, (1 - bit1) * quarter
    wave_coef, keep_at, send_at, low_near, low_half = lax.optimization_barrier(
        (wave_coef, keep_at, send_at, low_near, low_half))

    def begin(send):
        return swap(send.astype(F16), 0)

    def halve(keep, got):
        keep = keep + got.astype(F32)
        send = lax.dynamic_slice(keep, (send_at, zero), (quarter, size)).astype(F16)
        return send, lax.dynamic_slice(keep, (keep_at, zero), (quarter, size))

    def finish(keep, got):
        keep = keep + got.astype(F32)
        for stage in range(2, stages):
            send = keep.astype(F16)
            keep = send.astype(F32) + swap(send, stage).astype(F32)
        return keep.astype(F16)

    def gathered(piece):
        p3 = lax.ppermute(piece, BOTH, [(o * cols + c, (o ^ 3) * cols + c) for o in range(ops) for c in range(cols)])
        p1, p2 = swap(piece, 1), swap(piece, 0)
        near0, near1 = jnp.where(low_near, piece, p1), jnp.where(low_near, p1, piece)
        far0, far1 = jnp.where(low_near, p2, p3), jnp.where(low_near, p3, p2)
        return jnp.concatenate([
            jnp.where(low_half, near0, far0), jnp.where(low_half, near1, far1),
            jnp.where(low_half, far0, near0), jnp.where(low_half, far1, near1)], axis=0).astype(F32)

    vector = wave_coef
    own, weight = open_vector(wave_coef)
    mask = block_mask.reshape(-1)
    sent = operators(left, mask, blocks, True)
    for step in range(STEPS):
        other = across(own)
        weights = (weight, across(weight))
        part = own_part(own, right) if step else None
        inners, keeps, gots = [], [], []
        for c in range(CHUNKS):
            inner, send = sent_half(c, reach, weights, own, other, right, sent, part)
            gots.append(begin(send))
            inners.append(inner)
            own, other = lax.optimization_barrier((own, other, inner))[:2]
        inners[0], mask = lax.optimization_barrier((inners[0], mask, inners[-1]))[:2]
        if step == 0:
            kept = operators(left, mask, blocks, False)
        sigmas = []
        for c in range(CHUNKS):
            keep = kept_half(reach, weights, inners[c], kept)
            send, keep = halve(keep, gots[c])
            if c + 1 < CHUNKS:
                send, inners[c + 1] = lax.optimization_barrier((send, inners[c + 1]))
            sigmas.append(gathered(finish(keep, swap(send, 1))))
        corr = correlate(vector, sigmas)
        vector, weight, *own = correct(
            step == 0, step == STEPS - 1, reach, cells, vector, sigmas, diag_energy, (corr, across(corr)), weights)
        own = own[0] if own else None
    return normalise(cells, vector, (weight, across(weight)))


def solution(mesh):
    in_specs = (
        P("geom", "col"),
        P("geom", "col"),
        P(("geom", "op"), None, None),
        P(("geom", "op"), None, "col"),
        P(("geom", "op"), None, None),
    )
    body = functools.partial(local, mesh.shape["op"], mesh.shape["col"])
    return jax.shard_map(body, mesh=mesh, in_specs=in_specs, out_specs=P("geom", "col"), check_vma=False)
```

```python
import functools

import jax
import jax.numpy as jnp
from jax import lax
from jax.experimental import pallas as pl
from jax.experimental.pallas import tpu as pltpu
from jax.sharding import PartitionSpec as P

STEPS = 2
CHUNKS = 2
EPS = 1e-06
BLOCK = 16
TOP = 0.1875
BOTH = ("op", "col")
F32, F16, BF16 = jnp.float32, jnp.float16, jnp.bfloat16
SDS = jax.ShapeDtypeStruct
ANY = pl.BlockSpec(memory_space=pl.ANY)
VMEM = pl.BlockSpec(memory_space=pltpu.VMEM)
SMEM = pl.BlockSpec(memory_space=pltpu.SMEM)
ONE = SDS((8, 128), F32)
ORDER = ((2, 1), (1, 2))


def in_hbm(x):
    return pltpu.with_memory_space_constraint(x, pltpu.HBM)


def call(kernel, name, outs, out_specs, in_specs, args, flops, moved, scratch=(), mib=8):
    return pl.pallas_call(
        kernel, out_shape=outs, in_specs=in_specs, out_specs=out_specs, scratch_shapes=scratch, name=name,
        compiler_params=pltpu.CompilerParams(vmem_limit_bytes=mib * 2 ** 20),
        cost_estimate=pl.CostEstimate(flops=flops, bytes_accessed=moved, transcendentals=0))(*args)


def total(own_ref, other_ref):
    return own_ref[:1, :1] + other_ref[:1, :1]


def put(ref, parts):
    ref[...] = jnp.full(ref.shape, jnp.sum(parts), F32)


def folded(block):
    return jnp.sum(block.reshape(block.shape[0] // 8, 8, block.shape[1]), axis=0)


def scale_of(reach, weight):
    return 32768.0 / (reach * (jnp.sqrt(weight) + 1e-30))


def open_vector(coef):
    rows, cols = coef.shape
    parts = 8
    step = rows // parts

    def kernel(coef_ref, wave_ref, weight_ref, buf, sems):
        copies = []
        for p in range(parts):
            at = pl.ds(p * step, step)
            copies.append(pltpu.make_async_copy(coef_ref.at[at], buf.at[at], sems.at[p]))
            copies[-1].start()
        weight = jnp.zeros((8, cols), F32)
        for p in range(parts):
            copies[p].wait()
            for r in range(p * step, (p + 1) * step, BLOCK):
                block = buf[r:r + BLOCK, :]
                wave_ref[r:r + BLOCK, :] = block.astype(BF16)
                weight = weight + folded(block * block)
        put(weight_ref, weight)

    return call(kernel, "open_vector", (SDS((rows, cols), BF16), ONE), (VMEM, VMEM), [ANY], (in_hbm(coef),),
                3 * rows * cols, 8 * rows * cols,
                [pltpu.VMEM((rows, cols), F32), pltpu.SemaphoreType.DMA((parts,))], mib=12)


def first_half():
    me, core = lax.axis_index("op"), lax.axis_index("col")
    bit = 0
    for c, (mask, _) in enumerate(ORDER):
        place = me // mask + (me // 4 if mask == 2 else 0)
        bit = bit + jnp.where(core == c, place % 2, 0)
    return 1 - bit


def operators(left, mask, blocks, sent):
    pairs, width, _ = left.shape
    half, inside = width // 2, width // blocks
    strips = half // inside

    def kernel(mask_ref, left_ref, out_ref, buf, sems):
        h = first_half() if sent else 1 - first_half()
        order = [(k, i) for k in range(pairs) for i in range(strips)]
        copies = []
        for n, (k, i) in enumerate(order):
            copies.append(pltpu.make_async_copy(
                left_ref.at[k, pl.ds(pl.multiple_of(h * half + i * inside, inside), inside)], buf.at[n], sems.at[n]))
            copies[-1].start()
        for n, (k, i) in enumerate(order):
            copies[n].wait()
            for j in range(blocks):
                keep = mask_ref[(k * blocks + h * strips + i) * blocks + j]
                block = buf[n, :, j * inside:(j + 1) * inside]
                out_ref[i * inside:(i + 1) * inside, k * width + j * inside:k * width + (j + 1) * inside] = (
                    jnp.where(keep != 0, block, jnp.zeros_like(block)))

    count = pairs * strips
    return call(kernel, "sent_operators" if sent else "kept_operators", SDS((half, pairs * width), BF16), VMEM,
                [SMEM, ANY], (mask, in_hbm(left)), left.size, 2 * left.size,
                [pltpu.VMEM((count, inside, width), BF16), pltpu.SemaphoreType.DMA((count,))], mib=12)


def product(out_ref, scale, left_ref, right_ref, parts):
    step = left_ref.shape[0] // parts
    for p in range(parts):
        rows = slice(p * step, (p + 1) * step)
        out_ref[rows, :] = scale * jnp.dot(left_ref[rows, :], right_ref[...], preferred_element_type=F32)


def own_part(own, right):
    pairs, width, cols = right.shape
    step = width // 4

    def kernel(own_ref, right_ref, part_ref):
        here = pl.ds(pl.multiple_of(lax.axis_index("col") * cols, cols), cols)
        for k in range(pairs):
            near = right_ref[k, here, :]
            for r in range(0, width, step):
                part_ref[k * width + r:k * width + r + step, :] = jnp.dot(
                    own_ref[r:r + step, :], near, preferred_element_type=F32)

    return call(kernel, "own_part", SDS((pairs * width, cols), F32), VMEM, [VMEM] * 2, (own, right),
                2 * pairs * width * cols * cols, 2 ** 20)


def sent_half(chunk, reach, weights, own, other, right, masked, part):
    pairs, width, cols = right.shape
    size, half = cols // CHUNKS, width // 2
    at = slice(chunk * size, (chunk + 1) * size)
    step = width // 4

    def kernel(a_ref, b_ref, own_ref, other_ref, right_ref, masked_ref, inner_ref, send_ref):
        core = lax.axis_index("col")
        here = pl.ds(pl.multiple_of(core * cols, cols), cols)
        there = pl.ds(pl.multiple_of((1 - core) * cols, cols), cols)
        scale = scale_of(reach, total(a_ref, b_ref))
        for k in range(pairs):
            near, far = right_ref[k, here, at], right_ref[k, there, at]
            for r in range(0, width, step):
                rows = slice(k * width + r, k * width + r + step)
                inner_ref[rows, :] = (
                    (jnp.dot(own_ref[r:r + step, :], near, preferred_element_type=F32) if part is None
                     else own_ref[rows, at])
                    + jnp.dot(other_ref[r:r + step, :], far, preferred_element_type=F32)).astype(BF16)
        product(send_ref, scale, masked_ref, inner_ref, 2)

    return call(kernel, "sent_half_%d" % chunk, (SDS((pairs * width, size), BF16), SDS((half, size), F32)),
                (VMEM, VMEM), [VMEM] * 6,
                (*weights, own if part is None else part, other, right, masked),
                3 * pairs * width * width * size, 2 ** 20)


def kept_half(reach, weights, inner, masked):
    half, depth = masked.shape
    size = inner.shape[1]

    def kernel(a_ref, b_ref, inner_ref, masked_ref, keep_ref):
        product(keep_ref, scale_of(reach, total(a_ref, b_ref)), masked_ref, inner_ref, 2)

    return call(kernel, "kept_half", SDS((half, size), F32), VMEM, [VMEM] * 4,
                (*weights, inner, masked), 2 * half * depth * size, 2 ** 20)


def correlate(vector, sigmas):
    rows, cols = vector.shape
    size = cols // len(sigmas)

    def kernel(vector_ref, *refs):
        out = jnp.zeros((8, size), F32)
        for r in range(0, rows, BLOCK):
            for c, sigma_ref in enumerate(refs[:-1]):
                out = out + folded(vector_ref[r:r + BLOCK, c * size:(c + 1) * size] * sigma_ref[r:r + BLOCK, :])
        put(refs[-1], out)

    return call(kernel, "correlate", ONE, VMEM, [VMEM] * (1 + len(sigmas)), (vector, *sigmas), 2 * rows * cols, 2 ** 20)


def correct(first, last, reach, cells, vector, sigmas, diag, corr, weights):
    rows, cols = vector.shape
    size = cols // len(sigmas)

    def kernel(corr_a, corr_b, weight_a, weight_b, vector_ref, diag_ref, *refs):
        sigma_refs, (moved_ref, square_ref) = refs[:len(sigmas)], refs[len(sigmas):len(sigmas) + 2]
        weight = total(weight_a, weight_b)
        scale = scale_of(reach, weight)
        norm = jnp.ones((1, 1), F32) if first else lax.rsqrt(weight / cells + EPS)
        square = norm * norm
        theta = (total(corr_a, corr_b) / scale * square / cells) / (weight * square / cells + EPS)
        unit = norm / scale
        out = jnp.zeros((8, size), F32)
        for r in range(0, rows, BLOCK):
            for c, sigma_ref in enumerate(sigma_refs):
                at = (slice(r, r + BLOCK), slice(c * size, (c + 1) * size))
                coef = vector_ref[at] * norm
                spacing = diag_ref[at] - theta
                slope = spacing / jnp.maximum(spacing * spacing, 1.0)
                moved = coef - (sigma_ref[r:r + BLOCK, :] * unit - theta * coef) * slope
                moved_ref[at] = moved
                if not last:
                    refs[-1][at] = moved.astype(BF16)
                out = out + folded(moved * moved)
        put(square_ref, out)

    outs = (SDS((rows, cols), F32), ONE) + ((() if last else (SDS((rows, cols), BF16),)))
    return call(kernel, "correct", outs, (VMEM,) * len(outs), [VMEM] * (6 + len(sigmas)),
                (*corr, *weights, vector, diag, *sigmas), 12 * rows * cols, 2 ** 20)


def normalise(cells, vector, weights):
    rows, cols = vector.shape
    parts = 8
    step = rows // parts

    def kernel(weight_a, weight_b, vector_ref, out_ref, buf, sems):
        norm = lax.rsqrt(total(weight_a, weight_b) / cells + EPS)
        copies = []
        for p in range(parts):
            at = pl.ds(p * step, step)
            for r in range(p * step, (p + 1) * step, BLOCK):
                buf[r:r + BLOCK, :] = vector_ref[r:r + BLOCK, :] * norm
            copies.append(pltpu.make_async_copy(buf.at[at], out_ref.at[at], sems.at[p]))
            copies[-1].start()
        for copy in copies:
            copy.wait()

    return call(kernel, "normalise", SDS((rows, cols), F32), ANY, [VMEM] * 3, (*weights, vector),
                rows * cols, 8 * rows * cols, [pltpu.VMEM((rows, cols), F32), pltpu.SemaphoreType.DMA((parts,))])


def local(ops, cols, wave_coef, diag_energy, left, right, block_mask):
    pairs, width, _ = left.shape
    own_cols = right.shape[2]
    blocks = block_mask.shape[1]
    cells = float(width * width)
    half, quarter, size = width // 2, width // 4, own_cols // CHUNKS
    stages = ops.bit_length() - 1
    reach = float(pairs * ops * width) * TOP * TOP

    def swap(x, stage):
        pairing = []
        for o in range(ops):
            for c in range(cols):
                bit = (*ORDER[c % 2], 6)[stage] if stage < 3 else 1 << stage
                pairing.append((o * cols + c, (o ^ bit) * cols + c))
        return lax.ppermute(x, BOTH, pairing)

    def across(x):
        return lax.ppermute(x, "col", [(c, c ^ 1) for c in range(cols)])

    me, core = lax.axis_index("op").astype(jnp.uint32), lax.axis_index("col").astype(jnp.uint32)
    low, high = me & 1, ((me >> 1) ^ (me >> 2)) & 1
    bit0, bit1 = jnp.where(core == 0, high, low), jnp.where(core == 0, low, high)
    low_near, low_half, zero = bit1 == 0, bit0 == 0, jnp.zeros((), jnp.uint32)
    keep_at, send_at = bit1 * quarter, (1 - bit1) * quarter
    wave_coef, keep_at, send_at, low_near, low_half = lax.optimization_barrier(
        (wave_coef, keep_at, send_at, low_near, low_half))

    def begin(send):
        return swap(send.astype(F16), 0)

    def halve(keep, got):
        keep = keep + got.astype(F32)
        send = lax.dynamic_slice(keep, (send_at, zero), (quarter, size)).astype(F16)
        return send, lax.dynamic_slice(keep, (keep_at, zero), (quarter, size))

    def finish(keep, got):
        keep = keep + got.astype(F32)
        for stage in range(2, stages):
            send = keep.astype(F16)
            keep = send.astype(F32) + swap(send, stage).astype(F32)
        return keep.astype(F16)

    def gathered(piece):
        p3 = lax.ppermute(piece, BOTH, [(o * cols + c, (o ^ 3) * cols + c) for o in range(ops) for c in range(cols)])
        p1, p2 = swap(piece, 1), swap(piece, 0)
        near0, near1 = jnp.where(low_near, piece, p1), jnp.where(low_near, p1, piece)
        far0, far1 = jnp.where(low_near, p2, p3), jnp.where(low_near, p3, p2)
        return jnp.concatenate([
            jnp.where(low_half, near0, far0), jnp.where(low_half, near1, far1),
            jnp.where(low_half, far0, near0), jnp.where(low_half, far1, near1)], axis=0).astype(F32)

    vector = wave_coef
    own, weight = open_vector(wave_coef)
    mask = block_mask.reshape(-1)
    sent = operators(left, mask, blocks, True)
    for step in range(STEPS):
        other = across(own)
        weights = (weight, across(weight))
        part = own_part(own, right) if step else None
        inners, keeps, gots = [], [], []
        for c in range(CHUNKS):
            inner, send = sent_half(c, reach, weights, own, other, right, sent, part)
            gots.append(begin(send))
            inners.append(inner)
            own, other = lax.optimization_barrier((own, other, inner))[:2]
        inners[0], mask = lax.optimization_barrier((inners[0], mask, inners[-1]))[:2]
        if step == 0:
            kept = operators(left, mask, blocks, False)
        sigmas = []
        for c in range(CHUNKS):
            keep = kept_half(reach, weights, inners[c], kept)
            send, keep = halve(keep, gots[c])
            if c + 1 < CHUNKS:
                send, inners[c + 1] = lax.optimization_barrier((send, inners[c + 1]))
            sigmas.append(gathered(finish(keep, swap(send, 1))))
        corr = correlate(vector, sigmas)
        vector, weight, *own = correct(
            step == 0, step == STEPS - 1, reach, cells, vector, sigmas, diag_energy, (corr, across(corr)), weights)
        own = own[0] if own else None
    return normalise(cells, vector, (weight, across(weight)))


def solution(mesh):
    in_specs = (
        P("geom", "col"),
        P("geom", "col"),
        P(("geom", "op"), None, None),
        P(("geom", "op"), None, "col"),
        P(("geom", "op"), None, None),
    )
    body = functools.partial(local, mesh.shape["op"], mesh.shape["col"])
    return jax.shard_map(body, mesh=mesh, in_specs=in_specs, out_specs=P("geom", "col"), check_vma=False)
```
